512 devices in a mesh: pipe: 8 (over y_hi, core), mp: 64 (over z, x, y_lo).
Axes of the slice: x: 4, y: 8 (y_hi: 4, y_lo: 2; y = y_hi * 2 + y_lo), z: 8, core: 2. Of those that a mesh axis runs over, the one named last changes fastest.
Arguments:
- token_ids: int32 [8, 576], replicated, may hold values from 0 to 32767
- replica_table: int32 [8, 2], replicated, may hold values from 0 to 2, as said below
- embedding: bfloat16 [32768, 4096], P('pipe', 'mp'), may hold values from -150 to 150
- ln_gain: bfloat16 [8, 4096], P('pipe'), may hold values from 0.25 to 1.75
- ln_bias: bfloat16 [8, 4096], P('pipe'), may hold values from -3 to 3
- weight_in: bfloat16 [8, 12288, 4096], P('pipe', 'mp'), may hold values from -0.09375 to 0.09375
- weight_out: bfloat16 [8, 12288, 4096], P('pipe', 'mp'), may hold values from -0.0546875 to 0.0546875
- cotangent: bfloat16 [8, 576, 4096], P('pipe', None, 'mp'), may hold values from -0.1875 to 0.1875
Outputs:
- grad_in: bfloat16 [12288, 4096], P('mp', 'pipe')
- grad_out: bfloat16 [12288, 4096], P('mp', 'pipe')
The draws below stay inside these ranges and needn't reach their ends.
Inputs may be any that keep to these rules, and one draw needn't show every extreme that they name: `replica_table`: column 0 of a row is the replica's template: 0, 1 or 2: the first 8, 10 or 12 twelfths of the replica's 576 slots are live; some replica has template 2. Column 1 is 1 for a surviving replica and 0 for a failed one; at least one replica survives.
All inputs are finite; a program needn't handle non-finite values.
Results may differ from the reference program's by a relative error of at most 0.017.
Values may be sent and summed in bfloat16 or wider, within the bound.
No kernel may reach another device: no remote copies, remote signals or barrier semaphores. Data moves between devices by JAX's collectives and lax.ppermute only.
A program may use at most 64 MiB of HBM per device.

```python
import math
import jax
import jax.numpy as jnp
import numpy as np
from jax import lax

D = 4096
FF = 12288
VOCAB = 32768
TOK = 576
PIPES = 8


def draw_replica_table(key, part):
    key = jax.random.fold_in(key, 5)
    keys = jax.random.split(key, 4)
    replica_index = jnp.arange(PIPES, dtype=jnp.int32)
    template = jax.random.randint(keys[0], (PIPES,), 0, 3, dtype=jnp.int32)
    largest = jax.random.randint(keys[1], (), 0, PIPES, dtype=jnp.int32)
    template = jnp.where(replica_index == largest, 2, template)
    survived = jax.random.randint(keys[2], (PIPES,), 0, 2, dtype=jnp.int32)
    kept_one = jax.random.randint(keys[3], (), 0, PIPES, dtype=jnp.int32)
    survived = jnp.where(replica_index == kept_one, 1, survived)
    return jnp.stack([template, survived], axis=1).astype(jnp.int32)


def draw_embedding(key, part):
    key = jax.random.fold_in(key, 17)
    keys = jax.random.split(key, 3)
    column_pos = jnp.arange(D, dtype=jnp.float32) / D
    row_scale = jnp.exp(jax.random.uniform(keys[2], (VOCAB, 1), jnp.float32, 0.0, math.log(10.0)))
    jitter = jnp.exp(jax.random.uniform(keys[1], (D,), jnp.float32, 0.0, math.log(2.0)))
    raw_values = jnp.clip(jax.random.normal(keys[0], (VOCAB, D), jnp.float32), -4.0, 4.0)
    column_scale = jnp.exp(math.log(10.0) * column_pos) * jitter
    return (0.1 * raw_values * column_scale * row_scale).astype(jnp.bfloat16)


def place_ends(values, rng, smallest, high):
    longest = values.shape.index(max(values.shape))
    spots = []
    for shift in (0, 1):
        where = [jax.random.randint(jax.random.fold_in(rng, axis), (), 0, length) for axis, length in enumerate(values.shape)]
        where[longest] = (where[longest] + shift) % values.shape[longest]
        spots.append(tuple(where))
    return values.at[spots[0]].set(smallest).at[spots[1]].set(high)


def block_scale(rng, extent, cuts, low, high):
    loudness, own = 1.0, jax.random.fold_in(rng, 6)
    for position, blocks in cuts:
        heights = jnp.exp(jax.random.uniform(jax.random.fold_in(own, position), (blocks,), jnp.float32, low / len(cuts), high / len(cuts)))
        loudness = loudness * jnp.repeat(heights, extent[position] // blocks).reshape([-1 if axis == position else 1 for axis in range(len(extent))])
    return loudness


def rank_table(amount, skew):
    weights = [(1 << 20) // math.isqrt(rank ** skew) + 1 for rank in range(1, amount + 1)]
    width = 1 + sum(weights) // (1 << 30)
    return np.cumsum(np.array([max(1, weight // width) for weight in weights]))


def skewed_ids(stream_key, extent, amount, slope):
    listing = rank_table(amount, slope)
    ticket = jax.random.randint(jax.random.fold_in(stream_key, 1), extent, 0, int(listing[amount - 1]))
    rank = jnp.searchsorted(jnp.asarray(listing, jnp.int32), ticket, side="right")
    return jax.random.permutation(jax.random.fold_in(stream_key, 2), amount)[rank].astype(jnp.int32)


def centred(stream_key, shape, width, reach, shards=(), held_as=jnp.bfloat16):
    gain = block_scale(stream_key, shape, shards, -0.22, 0.18) if shards else 1.0
    result = jax.random.normal(stream_key, shape, jnp.float32) * width * gain
    return jnp.minimum(jnp.maximum(result, -reach), reach).astype(held_as)


def setup_inputs(seed: int = 0) -> dict:
    arg_keys = jax.random.split(jax.random.key(seed), 9)
    token_ids = place_ends(skewed_ids(arg_keys[0], (PIPES, TOK), VOCAB, 2), jax.random.fold_in(arg_keys[0], 3), 0, VOCAB - 1).astype(jnp.int32)
    replica_table = draw_replica_table(jax.random.fold_in(arg_keys[8], 71), 0)
    embedding = draw_embedding(jax.random.fold_in(arg_keys[8], 71), 0)
    ln_gain = jnp.clip(1.0 + 0.15 * jax.random.normal(arg_keys[3], (PIPES, D), jnp.float32), 0.25, 1.75).astype(jnp.bfloat16)
    ln_bias = centred(arg_keys[4], (PIPES, D), 0.5, 3.0, ((0, 8),))
    weight_in = centred(arg_keys[5], (PIPES, FF, D), D ** -0.5, 0.09375, ((0, 8), (1, 64)))
    weight_out = centred(arg_keys[6], (PIPES, FF, D), FF ** -0.5, 0.0546875, ((0, 8), (1, 64)))
    cotangent = centred(arg_keys[7], (PIPES, TOK, D), 0.03, 0.1875, ((0, 8), (2, 64)))
    return {"token_ids": token_ids, "replica_table": replica_table, "embedding": embedding, "ln_gain": ln_gain, "ln_bias": ln_bias, "weight_in": weight_in, "weight_out": weight_out, "cotangent": cotangent}


epsilon = 1e-05

def smooth_gate(values):
    return jax.nn.gelu(values, approximate=True)

def normalize(rows_in, gain_vec, bias_vec, full_width):
    row_mean = lax.optimization_barrier(jnp.sum(rows_in, axis=1, keepdims=True)) / full_width
    row_square = lax.optimization_barrier(jnp.sum(rows_in * rows_in, axis=1, keepdims=True)) / full_width
    scaled = (rows_in - row_mean) * lax.rsqrt(row_square - row_mean * row_mean + epsilon)
    return (scaled * gain_vec + bias_vec).astype(jnp.bfloat16)

def reference(token_ids, replica_table, embedding, ln_gain, ln_bias, weight_in, weight_out, cotangent):
    replica_index = jnp.arange(PIPES, dtype=jnp.int32)
    source_replica = jnp.min(jnp.where(replica_table[:, 1] == 1, replica_index, PIPES)).astype(jnp.int32)
    live_counts = (TOK * (4 + replica_table[:, 0]) // 6).astype(jnp.int32)
    first_proj = lax.dynamic_index_in_dim(weight_in, source_replica, 0, keepdims=False)
    second_proj = lax.dynamic_index_in_dim(weight_out, source_replica, 0, keepdims=False)
    gain_vec = lax.dynamic_index_in_dim(ln_gain, source_replica, 0, keepdims=False).astype(jnp.float32)
    bias_vec = lax.dynamic_index_in_dim(ln_bias, source_replica, 0, keepdims=False).astype(jnp.float32)
    row_index = jnp.arange(TOK, dtype=jnp.int32)

    def replica_step(totals, inputs):
        ids_row, cot_rows, live_count = inputs
        gathered = jnp.take(embedding, ids_row, axis=0).astype(jnp.float32)
        normed = normalize(gathered, gain_vec, bias_vec, D)
        preact = lax.dot_general(normed, first_proj, (((1,), (1,)), ((), ())), preferred_element_type=jnp.float32)
        activated = smooth_gate(preact).astype(jnp.bfloat16)
        upstream = jnp.where((row_index < live_count)[:, None], cot_rows, jnp.zeros_like(cot_rows))
        out_terms = jnp.dot(activated.T, upstream, preferred_element_type=jnp.float32).astype(jnp.bfloat16)
        act_grad = jnp.dot(upstream, second_proj.T, preferred_element_type=jnp.float32)
        pullback = jax.vjp(smooth_gate, preact)[1]
        dpreact = pullback(act_grad)[0].astype(jnp.bfloat16)
        in_terms = jnp.dot(dpreact.T, normed, preferred_element_type=jnp.float32).astype(jnp.bfloat16)
        return ((totals[0] + in_terms.astype(jnp.float32), totals[1] + out_terms.astype(jnp.float32)), None)
    start_in = jnp.zeros((FF, D), jnp.float32)
    start_out = jnp.zeros((FF, D), jnp.float32)
    totals, _ = lax.scan(replica_step, (start_in, start_out), (token_ids, cotangent, live_counts))
    return (totals[0].astype(jnp.bfloat16), totals[1].astype(jnp.bfloat16))
```

```python
import math

import jax
import jax.numpy as jnp
from jax import lax
from jax.experimental import pallas as pl
from jax.experimental.pallas import tpu as pltpu
from jax.sharding import Mesh, PartitionSpec as P

epsilon = 1e-05
bf16, f32 = jnp.bfloat16, jnp.float32
MIB = 1 << 20
SLOPE, CUBE = math.sqrt(2 / math.pi), 0.044715


def shift(value, axis, size, by):
    return lax.ppermute(value, axis, [(i, (i + by) % size) for i in range(size)])


def lookup_kernel(low_ref, high_ref, table_ref, out_ref, groups):
    width, vocab = table_ref.shape
    count = 8
    depth = vocab // count

    @pl.when(pl.program_id(0) == 0)
    def _():
        for k in range(count):
            groups[k * width:(k + 1) * width, :] = table_ref[:, k * depth:(k + 1) * depth]

    rows = out_ref.shape[0]
    place = lax.broadcasted_iota(jnp.int32, (rows, depth), 1)
    lane = lax.broadcasted_iota(jnp.int32, (rows, 2 * width), 1)
    total = jnp.zeros((rows, 2 * width), f32)
    for side, ref in enumerate((low_ref, high_ref)):
        ids = ref[...]
        group = jnp.right_shift(ids, 9)
        inner = jnp.bitwise_and(ids, depth - 1)
        hot = (place == inner).astype(f32).astype(bf16)
        picked = lax.dot_general(
            hot, groups[...], (((1,), (1,)), ((), ())), preferred_element_type=f32
        )
        pair = jnp.right_shift(group, 1)
        found = jnp.zeros((rows, 2 * width), f32)
        for j in range(count // 2):
            found += jnp.where(pair == j, picked[:, 2 * j * width:2 * (j + 1) * width], 0.0)
        turned = pltpu.roll(found, width, 1)
        found = jnp.where(jnp.bitwise_and(group, 1) == side, found, turned)
        total += jnp.where((lane >= width) == (side == 1), found, 0.0)
    out_ref[...] = total.astype(bf16)


def lookup(low, high, table):
    rows = low.shape[0]
    width, vocab = table.shape
    step = rows // 4
    return pl.pallas_call(
        lookup_kernel,
        grid=(4,),
        in_specs=[
            pl.BlockSpec((step, 1), lambda i: (i, 0)),
            pl.BlockSpec((step, 1), lambda i: (i, 0)),
            pl.BlockSpec((width, vocab), lambda i: (0, 0)),
        ],
        out_specs=pl.BlockSpec((step, 2 * width), lambda i: (i, 0)),
        out_shape=jax.ShapeDtypeStruct((rows, 2 * width), bf16),
        scratch_shapes=[pltpu.VMEM((8 * width, vocab // 8), bf16)],
        compiler_params=pltpu.CompilerParams(vmem_limit_bytes=32 * MIB),
        name="lookup",
    )(low, high, table)


def laid_out(info_ref, blocks):
    x = info_ref[0]
    own, right, left, far0, far1 = blocks
    depth, rows, lanes = own.shape
    half = depth // 2
    for k in range(depth):
        far = far0.at[k] if k < half else far1.at[k - half]
        for by, ref in ((0, own.at[k]), (3, right.at[k]), (1, left.at[k]), (2, far)):
            spot = 4 * k + jnp.bitwise_and(x + by, 3)
            yield ref, spot, pl.ds(pl.multiple_of(spot * lanes, lanes), lanes)


def unpacked(ref, start, step):
    rows, lanes = ref.shape
    half = lanes // 2
    first = ref[pl.ds(start, step), :].astype(f32)
    second = ref[pl.ds(rows // 2 + start, step), :].astype(f32)
    low = lax.broadcasted_iota(jnp.int32, (step, lanes), 1) < half
    return (
        jnp.where(low, first, pltpu.roll(second, half, 1)),
        jnp.where(low, pltpu.roll(first, half, 1), second),
    )


STEP = 48


def merge_kernel(info_ref, *refs):
    *blocks, out_ref = refs
    live, first = info_ref[1], info_ref[2]
    _, rows, lanes = blocks[0].shape

    @pl.loop(0, rows // 2 // STEP)
    def _(i):
        start = pl.multiple_of(i * STEP, STEP)
        slot = lax.broadcasted_iota(jnp.int32, (STEP, lanes), 0) + first + start
        for ref, _, here in laid_out(info_ref, blocks):
            for side, v in enumerate(unpacked(ref, start, STEP)):
                base = side * (rows // 2)
                v = jnp.where(slot + base < live, v, 0.0)
                out_ref[pl.ds(pl.multiple_of(base + start, STEP), STEP), here] = v.astype(bf16)


def norm_kernel(info_ref, *refs):
    *blocks, gain_ref, bias_ref, out_ref = refs
    _, rows, lanes = blocks[0].shape
    full = out_ref.shape[1]

    @pl.loop(0, rows // 2 // STEP)
    def _(i):
        start = pl.multiple_of(i * STEP, STEP)
        here = [pl.ds(pl.multiple_of(start + s * (rows // 2), STEP), STEP) for s in range(2)]
        zeros = jnp.zeros((STEP, lanes), f32)
        total, square = [zeros, zeros], [zeros, zeros]
        for ref, _, columns in laid_out(info_ref, blocks):
            for side, v in enumerate(unpacked(ref, start, STEP)):
                total[side] += v
                square[side] += v * v
                out_ref[here[side], columns] = v.astype(bf16)
        for side in range(2):
            mean = jnp.sum(total[side], axis=1, keepdims=True) / full
            power = jnp.sum(square[side], axis=1, keepdims=True) / full
            scale = lax.rsqrt(power - mean * mean + epsilon)
            for k in range(full // lanes):
                columns = slice(k * lanes, (k + 1) * lanes)
                v = (out_ref[here[side], columns].astype(f32) - mean) * scale
                v = v * gain_ref[k:k + 1, :] + bias_ref[k:k + 1, :]
                out_ref[here[side], columns] = v.astype(bf16)


def assemble(kernel, name, info, blocks, extra=()):
    depth, rows, lanes = blocks[0].shape
    return pl.pallas_call(
        kernel,
        in_specs=[pl.BlockSpec(memory_space=pltpu.SMEM)]
        + [pl.BlockSpec(memory_space=pltpu.VMEM)] * (len(blocks) + len(extra)),
        out_specs=pl.BlockSpec(memory_space=pltpu.VMEM),
        out_shape=jax.ShapeDtypeStruct((rows, 4 * depth * lanes), bf16),
        compiler_params=pltpu.CompilerParams(vmem_limit_bytes=32 * MIB),
        name=name,
    )(info, *blocks, *extra)


def gradient_kernel(normed0, normed1, up0, up1, weights, out_ref, acc, factors, ends):
    units, width = weights.shape[1:]
    rows = normed0.shape[0]
    tokens = ((normed0, up0), (normed1, up1))
    step = 1024
    for i, refs in enumerate(tokens):
        for j in range(2):
            total = jnp.zeros((rows, units), f32)
            for k in range(0, width, step):
                total += lax.dot_general(
                    refs[j][:, k:k + step], weights[j, :, k:k + step],
                    (((1,), (1,)), ((), ())), preferred_element_type=f32,
                )
            acc[j, i * rows:(i + 1) * rows, :] = total

    value = acc[0]
    bent = jnp.tanh(SLOPE * (value + CUBE * value * value * value))
    slope = 0.5 * (1.0 + bent) + 0.5 * value * (1.0 - bent * bent) * (
        SLOPE * (1.0 + 3.0 * CUBE * value * value)
    )
    factors[0] = jnp.transpose(acc[1] * slope).astype(bf16)
    factors[1] = jnp.transpose(0.5 * value * (1.0 + bent)).astype(bf16)

    main = 256
    rest = rows - main
    for j in range(2):
        for i, refs in enumerate(tokens):
            ends[j, i * rest:(i + 1) * rest, :] = refs[j][main:, :]

    out_width = out_ref.shape[-1]
    half = units // 2
    for q in range(width // out_width):
        columns = slice(q * out_width, (q + 1) * out_width)
        for j in range(2):
            end = jnp.concatenate([factors[j, :, main:rows], factors[j, :, rows + main:]], axis=1)
            total = jnp.dot(end, ends[j, :, columns], preferred_element_type=f32)
            for i, refs in enumerate(tokens):
                total += jnp.dot(
                    factors[j, :, i * rows:i * rows + main], refs[j][:main, columns],
                    preferred_element_type=f32,
                )
            total = total.astype(bf16)
            for y in range(2):
                out_ref[2 * q + y, j] = total[y * half:(y + 1) * half]


def gradients(normed, normed_other, upstream, upstream_other, weights):
    units, width = weights.shape[1:]
    rows = normed.shape[0]
    return pl.pallas_call(
        gradient_kernel,
        in_specs=[pl.BlockSpec(memory_space=pltpu.VMEM)] * 5,
        out_specs=pl.BlockSpec(memory_space=pltpu.VMEM),
        out_shape=jax.ShapeDtypeStruct((8, 2, units // 2, width // 4), bf16),
        scratch_shapes=[
            pltpu.VMEM((2, 2 * rows, units), f32),
            pltpu.VMEM((2, units, 2 * rows), bf16),
            pltpu.VMEM((2, 2 * (rows - 256), width), bf16),
        ],
        compiler_params=pltpu.CompilerParams(vmem_limit_bytes=48 * MIB),
        name="gradients",
    )(normed, normed_other, upstream, upstream_other, weights)


def gather_z(block):
    depth = lax.axis_size("z")
    return lax.all_to_all(jnp.broadcast_to(block, (depth,) + block.shape), "z", 0, 0)


def gather_x(own):
    return shift(own, "x", 4, 1), shift(own, "x", 4, -1)


def gather_far(right, left):
    half = right.shape[0] // 2
    return shift(right[:half], "x", 4, 1), shift(left[half:], "x", 4, -1)


def on_device(
    token_ids, replica_table, embedding, ln_gain, ln_bias, weight_in, weight_out, cotangent
):
    replicas = replica_table.shape[0]
    tok = cotangent.shape[1]
    cols = cotangent.shape[2]
    half = tok // 2
    vocab_block = embedding.shape[0]
    units, width = weight_in.shape[1:]
    part = units // 2

    yh, core, x, yl = (lax.axis_index(a) for a in ("yh", "core", "x", "yl"))
    position = 2 * yh + core
    replica_index = jnp.arange(replicas, dtype=jnp.int32)
    source = jnp.min(jnp.where(replica_table[:, 1] == 1, replica_index, replicas))
    live_counts = tok * (4 + replica_table[:, 0]) // 6
    live = lax.dynamic_index_in_dim(live_counts, position, 0, keepdims=False)

    pair = jnp.stack([weight_in[0], weight_out[0]]).reshape(2, 2, part, width)
    theirs = jnp.where(core == 0, pair[:, 1], pair[:, 0])
    mine = jnp.where(core == 0, pair[:, 0], pair[:, 1])
    mine = jnp.where(core == source % 2, mine, shift(theirs, "core", 2, 1))
    slot = jnp.arange(2).reshape(1, 2, 1, 1)
    spread = jnp.where((slot == yl) & (yh == source // 2), mine[:, None], jnp.zeros((), bf16))
    spread = spread.reshape(2, 2 * part, width)

    cot = cotangent[0].reshape(2, 2, half // 2, cols)
    cot = jnp.concatenate([cot[:, 0], cot[:, 1]], axis=2)
    cot = jnp.broadcast_to(cot, (8,) + cot.shape).reshape((16,) + cot.shape[1:])
    cot = lax.all_to_all(cot, ("z", "yl"), 0, 0).reshape(8, half, 2 * cols)

    local = (token_ids - position * vocab_block).reshape(replicas * 2, 2, half // 2)
    low = local[:, 0].reshape(-1, 1)
    high = local[:, 1].reshape(-1, 1)
    rows = lookup(low, high, embedding.T).reshape(2 * replicas, half // 2, 2 * cols)
    vectors = jnp.concatenate([ln_gain.reshape(-1, 2 * cols), ln_bias.reshape(-1, 2 * cols)])
    share = vectors.shape[0] // 2
    vectors = lax.dynamic_slice_in_dim(vectors, yl * share, share, 0)
    sent = jnp.concatenate(
        [rows, jnp.broadcast_to(vectors, (2 * replicas,) + vectors.shape)], axis=1
    )
    weights = lax.psum(spread, ("yh", "yl"))

    def slots(sent, cot):
        got = lax.all_to_all(sent, ("yh", "core", "yl"), 0, 0)
        info = jnp.stack([x, live, yl * half]).astype(jnp.int32)
        got, sides = lax.optimization_barrier((got, gather_x(cot)))
        upstream = assemble(merge_kernel, "merge", info, (cot, *sides, *gather_far(*sides)))
        upstream_other = shift(upstream, "core", 2, 1)
        got = got.reshape((replicas, 2) + got.shape[1:])
        emb = jnp.sum(got[:, :, : half // 2].astype(f32), axis=0).astype(bf16)
        emb = emb.reshape(half, 2 * cols)
        root = lax.dynamic_index_in_dim(got[:, :, half // 2 :], source, 0, keepdims=False)
        root = root.reshape(2, -1, 2 * cols).astype(f32)
        emb = gather_z(emb)
        sides = gather_x(emb)
        blocks = (emb, *sides, *gather_far(*sides))
        normed = assemble(norm_kernel, "norm", info, blocks, (root[0], root[1]))
        return normed, shift(normed, "core", 2, 1), upstream, upstream_other

    def nothing(sent, cot):
        return (jnp.zeros((half, width), bf16),) * 4

    normed, normed_other, upstream, upstream_other = lax.cond(
        source < replicas, slots, nothing, sent, cot
    )
    terms = gradients(normed, normed_other, upstream, upstream_other, weights)
    sums = lax.psum_scatter(terms, ("yh", "yl"), scatter_dimension=0)
    sums = sums.reshape(2, part, 2, width // 8)
    left, right = sums[:, :, 0], sums[:, :, 1]
    theirs = shift(jnp.where(core == 0, right, left), "core", 2, 1)
    mine = jnp.where(core == 0, left, right)
    top = jnp.where(core == 0, mine, theirs)
    bottom = jnp.where(core == 0, theirs, mine)
    done = jnp.concatenate([top, bottom], axis=1)
    return done[0], done[1]


def solution(mesh):
    fine = Mesh(mesh.devices.reshape(4, 2, 8, 4, 2), ("yh", "core", "z", "x", "yl"))
    pipe, mp = ("yh", "core"), ("z", "x", "yl")
    placed = (
        P(),
        P(),
        P(pipe, mp),
        P(pipe, None),
        P(pipe, None),
        P(pipe, mp, None),
        P(pipe, mp, None),
        P(pipe, None, mp),
    )
    return jax.shard_map(
        on_device,
        mesh=fine,
        in_specs=placed,
        out_specs=(P(mp, pipe), P(mp, pipe)),
        check_vma=False,
    )
```

```python
import math

import jax
import jax.numpy as jnp
from jax import lax
from jax.experimental import pallas as pl
from jax.experimental.pallas import tpu as pltpu
from jax.sharding import Mesh, PartitionSpec as P

epsilon = 1e-05
bf16, f32 = jnp.bfloat16, jnp.float32
MIB = 1 << 20
SLOPE, CUBE = math.sqrt(2 / math.pi), 0.044715


def shift(value, axis, size, by):
    return lax.ppermute(value, axis, [(i, (i + by) % size) for i in range(size)])


def lookup_kernel(low_ref, high_ref, own_ref, other_ref, out_ref, groups):
    width = own_ref.shape[0]
    count, depth = 8, groups.shape[1]

    @pl.when(pl.program_id(0) == 0)
    def _():
        for b, ref in enumerate((own_ref, other_ref)):
            for k in range(count):
                base = (b * count + k) * width
                groups[base:base + width, :] = ref[:, k * depth:(k + 1) * depth]

    rows = out_ref.shape[0]
    place = lax.broadcasted_iota(jnp.int32, (rows, depth), 1)
    lane = lax.broadcasted_iota(jnp.int32, (rows, 2 * width), 1)
    total = jnp.zeros((rows, 2 * width), f32)
    for side, ref in enumerate((low_ref, high_ref)):
        ids = ref[...]
        group = jnp.right_shift(ids, 9)
        inner = jnp.bitwise_and(ids, depth - 1)
        hot = (place == inner).astype(f32).astype(bf16)
        picked = lax.dot_general(
            hot, groups[...], (((1,), (1,)), ((), ())), preferred_element_type=f32
        )
        pair = jnp.right_shift(group, 1)
        found = jnp.zeros((rows, 2 * width), f32)
        for j in range(count):
            found += jnp.where(pair == j, picked[:, 2 * j * width:2 * (j + 1) * width], 0.0)
        turned = pltpu.roll(found, width, 1)
        found = jnp.where(jnp.bitwise_and(group, 1) == side, found, turned)
        total += jnp.where((lane >= width) == (side == 1), found, 0.0)
    out_ref[...] = total.astype(bf16)


def lookup(low, high, own, other, depth):
    rows = low.shape[0]
    width, lanes = own.shape
    step = rows // 2
    return pl.pallas_call(
        lookup_kernel,
        grid=(2,),
        in_specs=[
            pl.BlockSpec((step, 1), lambda i: (i, 0)),
            pl.BlockSpec((step, 1), lambda i: (i, 0)),
            pl.BlockSpec((width, lanes), lambda i: (0, 0)),
            pl.BlockSpec((width, lanes), lambda i: (0, 0)),
        ],
        out_specs=pl.BlockSpec((step, 2 * width), lambda i: (i, 0)),
        out_shape=jax.ShapeDtypeStruct((rows, 2 * width), bf16),
        scratch_shapes=[pltpu.VMEM((16 * width, depth), bf16)],
        compiler_params=pltpu.CompilerParams(vmem_limit_bytes=32 * MIB),
        name="lookup",
    )(low, high, own, other)


def laid_out(info_ref, blocks):
    x = info_ref[0]
    own, right, left, far0, far1 = blocks
    depth, rows, lanes = own.shape
    half = depth // 2
    for k in range(depth):
        far = far0.at[k] if k < half else far1.at[k - half]
        for by, ref in ((0, own.at[k]), (3, right.at[k]), (1, left.at[k]), (2, far)):
            spot = 4 * k + jnp.bitwise_and(x + by, 3)
            yield ref, spot, pl.ds(pl.multiple_of(spot * lanes, lanes), lanes)


def unpacked(ref, start, step):
    rows, lanes = ref.shape
    half = lanes // 2
    first = ref[pl.ds(start, step), :].astype(f32)
    second = ref[pl.ds(rows // 2 + start, step), :].astype(f32)
    low = lax.broadcasted_iota(jnp.int32, (step, lanes), 1) < half
    return (
        jnp.where(low, first, pltpu.roll(second, half, 1)),
        jnp.where(low, pltpu.roll(first, half, 1), second),
    )


STEP = 48


def merge_kernel(info_ref, *refs):
    *blocks, out_ref = refs
    live, first = info_ref[1], info_ref[2]
    _, rows, lanes = blocks[0].shape

    @pl.loop(0, rows // 2 // STEP)
    def _(i):
        start = pl.multiple_of(i * STEP, STEP)
        slot = lax.broadcasted_iota(jnp.int32, (STEP, lanes), 0) + first + start
        for ref, _, here in laid_out(info_ref, blocks):
            for side, v in enumerate(unpacked(ref, start, STEP)):
                base = side * (rows // 2)
                v = jnp.where(slot + base < live, v, 0.0)
                out_ref[pl.ds(pl.multiple_of(base + start, STEP), STEP), here] = v.astype(bf16)


def norm_kernel(info_ref, *refs):
    *blocks, gain_ref, bias_ref, out_ref = refs
    _, rows, lanes = blocks[0].shape
    full = out_ref.shape[1]

    @pl.loop(0, rows // 2 // STEP)
    def _(i):
        start = pl.multiple_of(i * STEP, STEP)
        here = [pl.ds(pl.multiple_of(start + s * (rows // 2), STEP), STEP) for s in range(2)]
        zeros = jnp.zeros((STEP, lanes), f32)
        total, square = [zeros, zeros], [zeros, zeros]
        for ref, _, columns in laid_out(info_ref, blocks):
            for side, v in enumerate(unpacked(ref, start, STEP)):
                total[side] += v
                square[side] += v * v
                out_ref[here[side], columns] = v.astype(bf16)
        for side in range(2):
            mean = jnp.sum(total[side], axis=1, keepdims=True) / full
            power = jnp.sum(square[side], axis=1, keepdims=True) / full
            scale = lax.rsqrt(power - mean * mean + epsilon)
            for k in range(full // lanes):
                columns = slice(k * lanes, (k + 1) * lanes)
                v = (out_ref[here[side], columns].astype(f32) - mean) * scale
                v = v * gain_ref[k:k + 1, :] + bias_ref[k:k + 1, :]
                out_ref[here[side], columns] = v.astype(bf16)


def assemble(kernel, name, info, blocks, extra=()):
    depth, rows, lanes = blocks[0].shape
    return pl.pallas_call(
        kernel,
        in_specs=[pl.BlockSpec(memory_space=pltpu.SMEM)]
        + [pl.BlockSpec(memory_space=pltpu.VMEM)] * (len(blocks) + len(extra)),
        out_specs=pl.BlockSpec(memory_space=pltpu.VMEM),
        out_shape=jax.ShapeDtypeStruct((rows, 4 * depth * lanes), bf16),
        compiler_params=pltpu.CompilerParams(vmem_limit_bytes=32 * MIB),
        name=name,
    )(info, *blocks, *extra)


def gradient_kernel(normed0, normed1, up0, up1, weights, out_ref, acc, factors, ends):
    units, width = weights.shape[1:]
    rows = normed0.shape[0]
    tokens = ((normed0, up0), (normed1, up1))
    step = 1024
    for i, refs in enumerate(tokens):
        for j in range(2):
            total = jnp.zeros((rows, units), f32)
            for k in range(0, width, step):
                total += lax.dot_general(
                    refs[j][:, k:k + step], weights[j, :, k:k + step],
                    (((1,), (1,)), ((), ())), preferred_element_type=f32,
                )
            acc[j, i * rows:(i + 1) * rows, :] = total

    value = acc[0]
    bent = jnp.tanh(SLOPE * (value + CUBE * value * value * value))
    slope = 0.5 * (1.0 + bent) + 0.5 * value * (1.0 - bent * bent) * (
        SLOPE * (1.0 + 3.0 * CUBE * value * value)
    )
    factors[0] = jnp.transpose(acc[1] * slope).astype(bf16)
    factors[1] = jnp.transpose(0.5 * value * (1.0 + bent)).astype(bf16)

    main = 256
    rest = rows - main
    for j in range(2):
        for i, refs in enumerate(tokens):
            ends[j, i * rest:(i + 1) * rest, :] = refs[j][main:, :]

    out_width = out_ref.shape[-1]
    half = units // 2
    for q in range(width // out_width):
        columns = slice(q * out_width, (q + 1) * out_width)
        for j in range(2):
            end = jnp.concatenate([factors[j, :, main:rows], factors[j, :, rows + main:]], axis=1)
            total = jnp.dot(end, ends[j, :, columns], preferred_element_type=f32)
            for i, refs in enumerate(tokens):
                total += jnp.dot(
                    factors[j, :, i * rows:i * rows + main], refs[j][:main, columns],
                    preferred_element_type=f32,
                )
            total = total.astype(bf16)
            for y in range(2):
                out_ref[2 * q + y, j] = total[y * half:(y + 1) * half]


def gradients(normed, normed_other, upstream, upstream_other, weights):
    units, width = weights.shape[1:]
    rows = normed.shape[0]
    return pl.pallas_call(
        gradient_kernel,
        in_specs=[pl.BlockSpec(memory_space=pltpu.VMEM)] * 5,
        out_specs=pl.BlockSpec(memory_space=pltpu.VMEM),
        out_shape=jax.ShapeDtypeStruct((8, 2, units // 2, width // 4), bf16),
        scratch_shapes=[
            pltpu.VMEM((2, 2 * rows, units), f32),
            pltpu.VMEM((2, units, 2 * rows), bf16),
            pltpu.VMEM((2, 2 * (rows - 256), width), bf16),
        ],
        compiler_params=pltpu.CompilerParams(vmem_limit_bytes=48 * MIB),
        name="gradients",
    )(normed, normed_other, upstream, upstream_other, weights)


def gather_z(block):
    depth = lax.axis_size("z")
    return lax.all_to_all(jnp.broadcast_to(block, (depth,) + block.shape), "z", 0, 0)


def gather_x(own):
    return shift(own, "x", 4, 1), shift(own, "x", 4, -1)


def gather_far(right, left):
    half = right.shape[0] // 2
    return shift(right[:half], "x", 4, 1), shift(left[half:], "x", 4, -1)


def on_device(
    token_ids, replica_table, embedding, ln_gain, ln_bias, weight_in, weight_out, cotangent
):
    replicas = replica_table.shape[0]
    tok = cotangent.shape[1]
    cols = cotangent.shape[2]
    half = tok // 2
    vocab_block = embedding.shape[0]
    units, width = weight_in.shape[1:]
    part = units // 2

    yh, core, x, yl = (lax.axis_index(a) for a in ("yh", "core", "x", "yl"))
    position = 2 * yh + core
    replica_index = jnp.arange(replicas, dtype=jnp.int32)
    source = jnp.min(jnp.where(replica_table[:, 1] == 1, replica_index, replicas))
    live_counts = tok * (4 + replica_table[:, 0]) // 6
    live = lax.dynamic_index_in_dim(live_counts, position, 0, keepdims=False)

    pair = jnp.stack([weight_in[0], weight_out[0]]).reshape(2, 2, part, width)
    theirs = jnp.where(core == 0, pair[:, 1], pair[:, 0])
    mine = jnp.where(core == 0, pair[:, 0], pair[:, 1])
    mine = jnp.where(core == source % 2, mine, shift(theirs, "core", 2, 1))
    slot = jnp.arange(2).reshape(1, 2, 1, 1)
    spread = jnp.where((slot == yl) & (yh == source // 2), mine[:, None], jnp.zeros((), bf16))
    spread = spread.reshape(2, 2 * part, width)

    cot = cotangent[0].reshape(2, 2, half // 2, cols)
    cot = jnp.concatenate([cot[:, 0], cot[:, 1]], axis=2)
    cot = jnp.broadcast_to(cot, (8,) + cot.shape).reshape((16,) + cot.shape[1:])

    vectors = jnp.concatenate([ln_gain.reshape(-1, 2 * cols), ln_bias.reshape(-1, 2 * cols)])
    share = vectors.shape[0] // 2
    held = jnp.concatenate([embedding.T, vectors], axis=1)
    ids = token_ids.reshape(4, 2, 2, 2, half // 2)
    ids = jnp.where(core == 0, ids[:, 0], ids[:, 1])
    local = jnp.bitwise_xor(ids - yh * 2 * vocab_block, core * vocab_block)
    low = local[:, :, 0].reshape(-1, 1)
    high = local[:, :, 1].reshape(-1, 1)
    weights = lax.psum(spread, ("yh", "yl"))

    def slots(low, high, held, cot):
        cot = lax.all_to_all(cot, ("z", "yl"), 0, 0).reshape(8, half, 2 * cols)
        swapped = shift(held, "core", 2, 1)
        rows = lookup(low, high, held, swapped, vocab_block // 8).reshape(8, half // 2, 2 * cols)
        vectors = jnp.where(core == source % 2, held[:, vocab_block:], swapped[:, vocab_block:])
        vectors = lax.dynamic_slice_in_dim(vectors, yl * share, share, 0)
        sent = jnp.concatenate([rows, jnp.broadcast_to(vectors, (8,) + vectors.shape)], axis=1)
        sent, cot = lax.optimization_barrier((sent, cot))
        got = lax.all_to_all(sent, ("yh", "yl"), 0, 0)
        info = jnp.stack([x, live, yl * half]).astype(jnp.int32)
        got, sides = lax.optimization_barrier((got, gather_x(cot)))
        far = gather_far(*sides)
        got = got.reshape((4, 2) + got.shape[1:])
        emb = jnp.sum(got[:, :, : half // 2].astype(f32), axis=0).astype(bf16)
        emb = emb.reshape(half, 2 * cols)
        root = lax.dynamic_index_in_dim(got[:, :, half // 2 :], source // 2, 0, keepdims=False)
        root = root.reshape(2, -1, 2 * cols).astype(f32)
        emb, far = lax.optimization_barrier((gather_z(emb), far))
        upstream = assemble(merge_kernel, "merge", info, (cot, *sides, *far))
        sides, upstream = lax.optimization_barrier((gather_x(emb), upstream))
        blocks = (emb, *sides, *gather_far(*sides))
        normed = assemble(norm_kernel, "norm", info, blocks, (root[0], root[1]))
        return normed, shift(normed, "core", 2, 1), upstream, shift(upstream, "core", 2, 1)

    def nothing(low, high, held, cot):
        return (jnp.zeros((half, width), bf16),) * 4

    normed, normed_other, upstream, upstream_other = lax.cond(
        source < replicas, slots, nothing, low, high, held, cot
    )
    terms = gradients(normed, normed_other, upstream, upstream_other, weights)
    sums = lax.psum_scatter(terms, ("yh", "yl"), scatter_dimension=0)
    sums = sums.reshape(2, part, 2, width // 8)
    left, right = sums[:, :, 0], sums[:, :, 1]
    theirs = shift(jnp.where(core == 0, right, left), "core", 2, 1)
    mine = jnp.where(core == 0, left, right)
    top = jnp.where(core == 0, mine, theirs)
    bottom = jnp.where(core == 0, theirs, mine)
    done = jnp.concatenate([top, bottom], axis=1)
    return done[0], done[1]


def solution(mesh):
    fine = Mesh(mesh.devices.reshape(4, 2, 8, 4, 2), ("yh", "core", "z", "x", "yl"))
    pipe, mp = ("yh", "core"), ("z", "x", "yl")
    placed = (
        P(),
        P(),
        P(pipe, mp),
        P(pipe, None),
        P(pipe, None),
        P(pipe, mp, None),
        P(pipe, mp, None),
        P(pipe, None, mp),
    )
    return jax.shard_map(
        on_device,
        mesh=fine,
        in_specs=placed,
        out_specs=(P(mp, pipe), P(mp, pipe)),
        check_vma=False,
    )
```

```python
import math

import jax
import jax.numpy as jnp
from jax import lax
from jax.experimental import pallas as pl
from jax.experimental.pallas import tpu as pltpu
from jax.sharding import Mesh, PartitionSpec as P

epsilon = 1e-05
bf16, f32 = jnp.bfloat16, jnp.float32
MIB = 1 << 20
SLOPE, CUBE = math.sqrt(2 / math.pi), 0.044715


def shift(value, axis, size, by):
    return lax.ppermute(value, axis, [(i, (i + by) % size) for i in range(size)])


def lookup_kernel(low_ref, high_ref, own_ref, other_ref, out_ref, groups):
    width = own_ref.shape[0]
    count, depth = 8, groups.shape[1]

    @pl.when(pl.program_id(0) == 0)
    def _():
        for b, ref in enumerate((own_ref, other_ref)):
            for k in range(count):
                base = (b * count + k) * width
                groups[base:base + width, :] = ref[:, k * depth:(k + 1) * depth]

    rows = out_ref.shape[0]
    place = lax.broadcasted_iota(jnp.int32, (rows, depth), 1)
    lane = lax.broadcasted_iota(jnp.int32, (rows, 2 * width), 1)
    total = jnp.zeros((rows, 2 * width), f32)
    for side, ref in enumerate((low_ref, high_ref)):
        ids = ref[...]
        group = jnp.right_shift(ids, 9)
        inner = jnp.bitwise_and(ids, depth - 1)
        hot = (place == inner).astype(f32).astype(bf16)
        picked = lax.dot_general(
            hot, groups[...], (((1,), (1,)), ((), ())), preferred_element_type=f32
        )
        pair = jnp.right_shift(group, 1)
        found = jnp.zeros((rows, 2 * width), f32)
        for j in range(count):
            found += jnp.where(pair == j, picked[:, 2 * j * width:2 * (j + 1) * width], 0.0)
        turned = pltpu.roll(found, width, 1)
        found = jnp.where(jnp.bitwise_and(group, 1) == side, found, turned)
        total += jnp.where((lane >= width) == (side == 1), found, 0.0)
    out_ref[...] = total.astype(bf16)


def lookup(low, high, own, other, depth):
    rows = low.shape[0]
    width, lanes = own.shape
    step = rows // 2
    return pl.pallas_call(
        lookup_kernel,
        grid=(2,),
        in_specs=[
            pl.BlockSpec((step, 1), lambda i: (i, 0)),
            pl.BlockSpec((step, 1), lambda i: (i, 0)),
            pl.BlockSpec((width, lanes), lambda i: (0, 0)),
            pl.BlockSpec((width, lanes), lambda i: (0, 0)),
        ],
        out_specs=pl.BlockSpec((step, 2 * width), lambda i: (i, 0)),
        out_shape=jax.ShapeDtypeStruct((rows, 2 * width), bf16),
        scratch_shapes=[pltpu.VMEM((16 * width, depth), bf16)],
        compiler_params=pltpu.CompilerParams(vmem_limit_bytes=32 * MIB),
        name="lookup",
    )(low, high, own, other)


def laid_out(info_ref, blocks):
    x = info_ref[0]
    own, right, left, far0, far1 = blocks
    depth, rows, lanes = own.shape
    half = depth // 2
    for k in range(depth):
        far = far0.at[k] if k < half else far1.at[k - half]
        for by, ref in ((0, own.at[k]), (3, right.at[k]), (1, left.at[k]), (2, far)):
            spot = 4 * k + jnp.bitwise_and(x + by, 3)
            yield ref, spot, pl.ds(pl.multiple_of(spot * lanes, lanes), lanes)


def unpacked(ref, start, step):
    rows, lanes = ref.shape
    half = lanes // 2
    first = ref[pl.ds(start, step), :].astype(f32)
    second = ref[pl.ds(rows // 2 + start, step), :].astype(f32)
    low = lax.broadcasted_iota(jnp.int32, (step, lanes), 1) < half
    return (
        jnp.where(low, first, pltpu.roll(second, half, 1)),
        jnp.where(low, pltpu.roll(first, half, 1), second),
    )


STEP = 48


def merge_kernel(info_ref, *refs):
    *blocks, out_ref = refs
    live, first = info_ref[1], info_ref[2]
    _, rows, lanes = blocks[0].shape

    @pl.loop(0, rows // 2 // STEP)
    def _(i):
        start = pl.multiple_of(i * STEP, STEP)
        slot = lax.broadcasted_iota(jnp.int32, (STEP, lanes), 0) + first + start
        for ref, _, here in laid_out(info_ref, blocks):
            for side, v in enumerate(unpacked(ref, start, STEP)):
                base = side * (rows // 2)
                v = jnp.where(slot + base < live, v, 0.0)
                out_ref[pl.ds(pl.multiple_of(base + start, STEP), STEP), here] = v.astype(bf16)


def norm_kernel(info_ref, *refs):
    *blocks, gain_ref, bias_ref, out_ref = refs
    _, rows, lanes = blocks[0].shape
    full = out_ref.shape[1]

    @pl.loop(0, rows // 2 // STEP)
    def _(i):
        start = pl.multiple_of(i * STEP, STEP)
        here = [pl.ds(pl.multiple_of(start + s * (rows // 2), STEP), STEP) for s in range(2)]
        zeros = jnp.zeros((STEP, lanes), f32)
        total, square = [zeros, zeros], [zeros, zeros]
        for ref, _, columns in laid_out(info_ref, blocks):
            for side, v in enumerate(unpacked(ref, start, STEP)):
                total[side] += v
                square[side] += v * v
                out_ref[here[side], columns] = v.astype(bf16)
        for side in range(2):
            mean = jnp.sum(total[side], axis=1, keepdims=True) / full
            power = jnp.sum(square[side], axis=1, keepdims=True) / full
            scale = lax.rsqrt(power - mean * mean + epsilon)
            for k in range(full // lanes):
                columns = slice(k * lanes, (k + 1) * lanes)
                v = (out_ref[here[side], columns].astype(f32) - mean) * scale
                v = v * gain_ref[k:k + 1, :] + bias_ref[k:k + 1, :]
                out_ref[here[side], columns] = v.astype(bf16)


def assemble(kernel, name, info, blocks, extra=()):
    depth, rows, lanes = blocks[0].shape
    return pl.pallas_call(
        kernel,
        in_specs=[pl.BlockSpec(memory_space=pltpu.SMEM)]
        + [pl.BlockSpec(memory_space=pltpu.VMEM)] * (len(blocks) + len(extra)),
        out_specs=pl.BlockSpec(memory_space=pltpu.VMEM),
        out_shape=jax.ShapeDtypeStruct((rows, 4 * depth * lanes), bf16),
        compiler_params=pltpu.CompilerParams(vmem_limit_bytes=32 * MIB),
        name=name,
    )(info, *blocks, *extra)


def stage_kernel(flag_ref, first_ref, second_ref, out_ref):
    rows = first_ref.shape[0]
    for j, ref in enumerate((first_ref, second_ref)):
        kept = jnp.where(flag_ref[0] == 1, ref[...].astype(f32), 0.0)
        out_ref[0, j * rows:(j + 1) * rows, :] = kept.astype(bf16)


def stage(flag, first, second):
    units, width = first.shape
    block = pl.BlockSpec((units // 2, width // 4), lambda i: (i % 2, i // 2))
    return pl.pallas_call(
        stage_kernel,
        grid=(8,),
        in_specs=[pl.BlockSpec(memory_space=pltpu.SMEM), block, block],
        out_specs=pl.BlockSpec((1, units, width // 4), lambda i: (i, 0, 0)),
        out_shape=jax.ShapeDtypeStruct((8, units, width // 4), bf16),
        compiler_params=pltpu.CompilerParams(vmem_limit_bytes=32 * MIB),
        name="stage",
    )(flag, first, second)


def gradient_kernel(normed0, normed1, up0, up1, weights, out_ref, acc, factors, ends):
    units = weights.shape[1]
    rows, width = normed0.shape
    tokens = ((normed0, up0), (normed1, up1))
    half, step = units // 2, width // 4
    for i, refs in enumerate(tokens):
        for j in range(2):
            total = jnp.zeros((rows, units), f32)
            for k in range(4):
                both = [weights[2 * k + y, j * half:(j + 1) * half, :] for y in range(2)]
                total += lax.dot_general(
                    refs[j][:, k * step:(k + 1) * step], jnp.concatenate(both),
                    (((1,), (1,)), ((), ())), preferred_element_type=f32,
                )
            acc[j, i * rows:(i + 1) * rows, :] = total

    value = acc[0]
    bent = jnp.tanh(SLOPE * (value + CUBE * value * value * value))
    slope = 0.5 * (1.0 + bent) + 0.5 * value * (1.0 - bent * bent) * (
        SLOPE * (1.0 + 3.0 * CUBE * value * value)
    )
    factors[0] = jnp.transpose(acc[1] * slope).astype(bf16)
    factors[1] = jnp.transpose(0.5 * value * (1.0 + bent)).astype(bf16)

    main = 256
    rest = rows - main
    for j in range(2):
        for i, refs in enumerate(tokens):
            ends[j, i * rest:(i + 1) * rest, :] = refs[j][main:, :]

    out_width = out_ref.shape[-1]
    for q in range(width // out_width):
        columns = slice(q * out_width, (q + 1) * out_width)
        for j in range(2):
            end = jnp.concatenate([factors[j, :, main:rows], factors[j, :, rows + main:]], axis=1)
            total = jnp.dot(end, ends[j, :, columns], preferred_element_type=f32)
            for i, refs in enumerate(tokens):
                total += jnp.dot(
                    factors[j, :, i * rows:i * rows + main], refs[j][:main, columns],
                    preferred_element_type=f32,
                )
            total = total.astype(bf16)
            for y in range(2):
                out_ref[2 * q + y, j] = total[y * half:(y + 1) * half]


def gradients(normed, normed_other, upstream, upstream_other, weights):
    units = weights.shape[1]
    rows, width = normed.shape
    return pl.pallas_call(
        gradient_kernel,
        in_specs=[pl.BlockSpec(memory_space=pltpu.VMEM)] * 5,
        out_specs=pl.BlockSpec(memory_space=pltpu.VMEM),
        out_shape=jax.ShapeDtypeStruct((8, 2, units // 2, width // 4), bf16),
        scratch_shapes=[
            pltpu.VMEM((2, 2 * rows, units), f32),
            pltpu.VMEM((2, units, 2 * rows), bf16),
            pltpu.VMEM((2, 2 * (rows - 256), width), bf16),
        ],
        compiler_params=pltpu.CompilerParams(vmem_limit_bytes=48 * MIB),
        name="gradients",
    )(normed, normed_other, upstream, upstream_other, weights)


def gather_z(block):
    depth = lax.axis_size("z")
    return lax.all_to_all(jnp.broadcast_to(block, (depth,) + block.shape), "z", 0, 0)


def gather_x(own):
    return shift(own, "x", 4, 1), shift(own, "x", 4, -1)


def gather_far(right, left):
    half = right.shape[0] // 2
    return shift(right[:half], "x", 4, 1), shift(left[half:], "x", 4, -1)


def on_device(
    token_ids, replica_table, embedding, ln_gain, ln_bias, weight_in, weight_out, cotangent
):
    replicas = replica_table.shape[0]
    tok = cotangent.shape[1]
    cols = cotangent.shape[2]
    half = tok // 2
    vocab_block = embedding.shape[0]
    units, width = weight_in.shape[1:]
    part = units // 2

    yh, core, x, yl = (lax.axis_index(a) for a in ("yh", "core", "x", "yl"))
    position = 2 * yh + core
    replica_index = jnp.arange(replicas, dtype=jnp.int32)
    source = jnp.min(jnp.where(replica_table[:, 1] == 1, replica_index, replicas))
    live_counts = tok * (4 + replica_table[:, 0]) // 6
    live = lax.dynamic_index_in_dim(live_counts, position, 0, keepdims=False)

    flag = (position == source).astype(jnp.int32).reshape(1)
    share_w = lax.psum_scatter(
        stage(flag, weight_in[0], weight_out[0]), ("yh", "core"), scatter_dimension=0
    )

    cot = cotangent[0].reshape(2, 2, half // 2, cols)
    cot = jnp.concatenate([cot[:, 0], cot[:, 1]], axis=2)
    cot = jnp.broadcast_to(cot, (8,) + cot.shape).reshape((16,) + cot.shape[1:])

    vectors = jnp.concatenate([ln_gain.reshape(-1, 2 * cols), ln_bias.reshape(-1, 2 * cols)])
    share = vectors.shape[0] // 2
    held = jnp.concatenate([embedding.T, vectors], axis=1)
    ids = token_ids.reshape(4, 2, 2, 2, half // 2)
    ids = jnp.where(core == 0, ids[:, 0], ids[:, 1])
    local = jnp.bitwise_xor(ids - yh * 2 * vocab_block, core * vocab_block)
    low = local[:, :, 0].reshape(-1, 1)
    high = local[:, :, 1].reshape(-1, 1)

    info = jnp.stack([x, live, yl * half]).astype(jnp.int32)

    def slots(low, high, held, cot):
        cot = lax.all_to_all(cot, ("z", "yl"), 0, 0).reshape(8, half, 2 * cols)
        swapped = shift(held, "core", 2, 1)
        rows = lookup(low, high, held, swapped, vocab_block // 8).reshape(8, half // 2, 2 * cols)
        vectors = jnp.where(core == source % 2, held[:, vocab_block:], swapped[:, vocab_block:])
        vectors = lax.dynamic_slice_in_dim(vectors, yl * share, share, 0)
        sent = jnp.concatenate([rows, jnp.broadcast_to(vectors, (8,) + vectors.shape)], axis=1)
        sent, cot = lax.optimization_barrier((sent, cot))
        got = lax.all_to_all(sent, ("yh", "yl"), 0, 0)
        got, sides = lax.optimization_barrier((got, gather_x(cot)))
        far = gather_far(*sides)
        got = got.reshape((4, 2) + got.shape[1:])
        emb = jnp.sum(got[:, :, : half // 2].astype(f32), axis=0).astype(bf16)
        emb = emb.reshape(half, 2 * cols)
        root = lax.dynamic_index_in_dim(got[:, :, half // 2 :], source // 2, 0, keepdims=False)
        root = root.reshape(2, -1, 2 * cols).astype(f32)
        return (root[0], root[1], gather_z(emb), cot, *sides, *far)

    def no_slots(low, high, held, cot):
        lanes = 2 * cols
        vector, blocks = jnp.zeros((width // lanes, lanes), f32), jnp.zeros((8, half, lanes), bf16)
        return (vector, vector) + (blocks,) * 4 + (blocks[:4],) * 2

    def features(gain, bias, emb, *cot):
        upstream = assemble(merge_kernel, "merge", info, cot)
        sides, upstream = lax.optimization_barrier((gather_x(emb), upstream))
        blocks = (emb, *sides, *gather_far(*sides))
        normed = assemble(norm_kernel, "norm", info, blocks, (gain, bias))
        return normed, shift(normed, "core", 2, 1), upstream, shift(upstream, "core", 2, 1)

    def no_features(*blocks):
        return (jnp.zeros((half, width), bf16),) * 4

    some = source < replicas
    blocks = lax.cond(some, slots, no_slots, low, high, held, cot)
    *blocks, share_w = lax.optimization_barrier((*blocks, share_w))
    weights = lax.all_gather(share_w, ("yh", "yl"))
    normed, normed_other, upstream, upstream_other = lax.cond(some, features, no_features, *blocks)
    terms = gradients(normed, normed_other, upstream, upstream_other, weights)
    sums = lax.psum_scatter(terms, ("yh", "yl"), scatter_dimension=0)
    sums = sums.reshape(2, part, 2, width // 8)
    left, right = sums[:, :, 0], sums[:, :, 1]
    theirs = shift(jnp.where(core == 0, right, left), "core", 2, 1)
    mine = jnp.where(core == 0, left, right)
    top = jnp.where(core == 0, mine, theirs)
    bottom = jnp.where(core == 0, theirs, mine)
    done = jnp.concatenate([top, bottom], axis=1)
    return done[0], done[1]


def solution(mesh):
    fine = Mesh(mesh.devices.reshape(4, 2, 8, 4, 2), ("yh", "core", "z", "x", "yl"))
    pipe, mp = ("yh", "core"), ("z", "x", "yl")
    placed = (
        P(),
        P(),
        P(pipe, mp),
        P(pipe, None),
        P(pipe, None),
        P(pipe, mp, None),
        P(pipe, mp, None),
        P(pipe, None, mp),
    )
    return jax.shard_map(
        on_device,
        mesh=fine,
        in_specs=placed,
        out_specs=(P(mp, pipe), P(mp, pipe)),
        check_vma=False,
    )
```

```python
import math

import jax
import jax.numpy as jnp
from jax import lax
from jax.experimental import pallas as pl
from jax.experimental.pallas import tpu as pltpu
from jax.sharding import Mesh, PartitionSpec as P

epsilon = 1e-05
bf16, f32 = jnp.bfloat16, jnp.float32
MIB = 1 << 20
SLOPE, CUBE = math.sqrt(2 / math.pi), 0.044715


def shift(value, axis, size, by):
    return lax.ppermute(value, axis, [(i, (i + by) % size) for i in range(size)])


def lookup_kernel(low_ref, high_ref, own_ref, other_ref, out_ref, groups):
    width = own_ref.shape[0]
    count, depth = 8, groups.shape[1]

    @pl.when(pl.program_id(0) == 0)
    def _():
        for b, ref in enumerate((own_ref, other_ref)):
            for k in range(count):
                base = (b * count + k) * width
                groups[base:base + width, :] = ref[:, k * depth:(k + 1) * depth]

    rows = out_ref.shape[0]
    place = lax.broadcasted_iota(jnp.int32, (rows, depth), 1)
    lane = lax.broadcasted_iota(jnp.int32, (rows, 2 * width), 1)
    total = jnp.zeros((rows, 2 * width), f32)
    for side, ref in enumerate((low_ref, high_ref)):
        ids = ref[...]
        group = jnp.right_shift(ids, 9)
        inner = jnp.bitwise_and(ids, depth - 1)
        hot = (place == inner).astype(f32).astype(bf16)
        picked = lax.dot_general(
            hot, groups[...], (((1,), (1,)), ((), ())), preferred_element_type=f32
        )
        pair = jnp.right_shift(group, 1)
        found = jnp.zeros((rows, 2 * width), f32)
        for j in range(count):
            found += jnp.where(pair == j, picked[:, 2 * j * width:2 * (j + 1) * width], 0.0)
        turned = pltpu.roll(found, width, 1)
        found = jnp.where(jnp.bitwise_and(group, 1) == side, found, turned)
        total += jnp.where((lane >= width) == (side == 1), found, 0.0)
    out_ref[...] = total.astype(bf16)


def lookup(low, high, own, other, depth):
    rows = low.shape[0]
    width, lanes = own.shape
    step = rows // 2
    return pl.pallas_call(
        lookup_kernel,
        grid=(2,),
        in_specs=[
            pl.BlockSpec((step, 1), lambda i: (i, 0)),
            pl.BlockSpec((step, 1), lambda i: (i, 0)),
            pl.BlockSpec((width, lanes), lambda i: (0, 0)),
            pl.BlockSpec((width, lanes), lambda i: (0, 0)),
        ],
        out_specs=pl.BlockSpec((step, 2 * width), lambda i: (i, 0)),
        out_shape=jax.ShapeDtypeStruct((rows, 2 * width), bf16),
        scratch_shapes=[pltpu.VMEM((16 * width, depth), bf16)],
        compiler_params=pltpu.CompilerParams(vmem_limit_bytes=32 * MIB),
        name="lookup",
    )(low, high, own, other)


def laid_out(info_ref, blocks):
    x = info_ref[0]
    own, right, left, far0, far1 = blocks
    depth, rows, lanes = own.shape
    half = depth // 2
    for k in range(depth):
        far = far0.at[k] if k < half else far1.at[k - half]
        for by, ref in ((0, own.at[k]), (3, right.at[k]), (1, left.at[k]), (2, far)):
            spot = 4 * k + jnp.bitwise_and(x + by, 3)
            yield ref, spot, pl.ds(pl.multiple_of(spot * lanes, lanes), lanes)


def unpacked(ref, start, step):
    rows, lanes = ref.shape
    half = lanes // 2
    first = ref[pl.ds(start, step), :].astype(f32)
    second = ref[pl.ds(rows // 2 + start, step), :].astype(f32)
    low = lax.broadcasted_iota(jnp.int32, (step, lanes), 1) < half
    return (
        jnp.where(low, first, pltpu.roll(second, half, 1)),
        jnp.where(low, pltpu.roll(first, half, 1), second),
    )


STEP = 48


def merge_kernel(info_ref, *refs):
    *blocks, out_ref = refs
    live, first = info_ref[1], info_ref[2]
    _, rows, lanes = blocks[0].shape

    @pl.loop(0, rows // 2 // STEP)
    def _(i):
        start = pl.multiple_of(i * STEP, STEP)
        slot = lax.broadcasted_iota(jnp.int32, (STEP, lanes), 0) + first + start
        for ref, _, here in laid_out(info_ref, blocks):
            for side, v in enumerate(unpacked(ref, start, STEP)):
                base = side * (rows // 2)
                v = jnp.where(slot + base < live, v, 0.0)
                out_ref[pl.ds(pl.multiple_of(base + start, STEP), STEP), here] = v.astype(bf16)


def norm_kernel(info_ref, *refs):
    *blocks, gain_ref, bias_ref, out_ref = refs
    _, rows, lanes = blocks[0].shape
    full = out_ref.shape[1]

    @pl.loop(0, rows // 2 // STEP)
    def _(i):
        start = pl.multiple_of(i * STEP, STEP)
        here = [pl.ds(pl.multiple_of(start + s * (rows // 2), STEP), STEP) for s in range(2)]
        zeros = jnp.zeros((STEP, lanes), f32)
        total, square = [zeros, zeros], [zeros, zeros]
        for ref, _, columns in laid_out(info_ref, blocks):
            for side, v in enumerate(unpacked(ref, start, STEP)):
                total[side] += v
                square[side] += v * v
                out_ref[here[side], columns] = v.astype(bf16)
        for side in range(2):
            mean = jnp.sum(total[side], axis=1, keepdims=True) / full
            power = jnp.sum(square[side], axis=1, keepdims=True) / full
            scale = lax.rsqrt(power - mean * mean + epsilon)
            for k in range(full // lanes):
                columns = slice(k * lanes, (k + 1) * lanes)
                v = (out_ref[here[side], columns].astype(f32) - mean) * scale
                v = v * gain_ref[k:k + 1, :] + bias_ref[k:k + 1, :]
                out_ref[here[side], columns] = v.astype(bf16)


def assemble(kernel, name, info, blocks, extra=()):
    depth, rows, lanes = blocks[0].shape
    return pl.pallas_call(
        kernel,
        in_specs=[pl.BlockSpec(memory_space=pltpu.SMEM)]
        + [pl.BlockSpec(memory_space=pltpu.VMEM)] * (len(blocks) + len(extra)),
        out_specs=pl.BlockSpec(memory_space=pltpu.VMEM),
        out_shape=jax.ShapeDtypeStruct((rows, 4 * depth * lanes), bf16),
        compiler_params=pltpu.CompilerParams(vmem_limit_bytes=32 * MIB),
        name=name,
    )(info, *blocks, *extra)


def stage_kernel(flag_ref, first_ref, second_ref, out_ref):
    rows = first_ref.shape[0]
    for j, ref in enumerate((first_ref, second_ref)):
        kept = jnp.where(flag_ref[0] == 1, ref[...].astype(f32), 0.0)
        out_ref[0, j * rows:(j + 1) * rows, :] = kept.astype(bf16)


def stage(flag, first, second):
    units, width = first.shape
    block = pl.BlockSpec((units // 2, width // 4), lambda i: (i % 2, i // 2))
    return pl.pallas_call(
        stage_kernel,
        grid=(8,),
        in_specs=[pl.BlockSpec(memory_space=pltpu.SMEM), block, block],
        out_specs=pl.BlockSpec((1, units, width // 4), lambda i: (i, 0, 0)),
        out_shape=jax.ShapeDtypeStruct((8, units, width // 4), bf16),
        compiler_params=pltpu.CompilerParams(vmem_limit_bytes=60 * MIB),
        name="stage",
    )(flag, first, second)


def gradient_kernel(
    normed0, normed1, up0, up1, weights, out, rows0, rows1, rows2, rows3, held, done, acc, factors,
    come, go,
):
    units, step = weights.shape[1:]
    rows = normed0.shape[0]
    tokens = ((rows0, rows2), (rows1, rows3))
    half = units // 2
    main = 256

    copies = []
    for k in range(4):
        columns = pl.ds(k * step, step)
        pairs = [(weights.at[pl.ds(2 * k, 2)], held.at[pl.ds(2 * k, 2)])]
        for source, target in ((normed0, rows0), (normed1, rows1), (up0, rows2), (up1, rows3)):
            pairs.append((source.at[:, columns], target.at[:, columns]))
        copies.append(
            [pltpu.make_async_copy(a, b, come.at[k, n]) for n, (a, b) in enumerate(pairs)]
        )
        for copy in copies[k]:
            copy.start()

    for k in range(4):
        for copy in copies[k]:
            copy.wait()
        for j in range(2):
            both = jnp.concatenate(
                [held[2 * k + y, j * half:(j + 1) * half, :] for y in range(2)]
            )
            for t, refs in enumerate(tokens):
                here = (j, slice(t * rows, (t + 1) * rows))
                term = lax.dot_general(
                    refs[j][:, k * step:(k + 1) * step], both, (((1,), (1,)), ((), ())),
                    preferred_element_type=f32,
                )
                acc[here] = term if k == 0 else acc[here] + term

    value = acc[0]
    bent = jnp.tanh(SLOPE * (value + CUBE * value * value * value))
    slope = 0.5 * (1.0 + bent) + 0.5 * value * (1.0 - bent * bent) * (
        SLOPE * (1.0 + 3.0 * CUBE * value * value)
    )
    factors[0] = jnp.transpose(acc[1] * slope).astype(bf16)
    factors[1] = jnp.transpose(0.5 * value * (1.0 + bent)).astype(bf16)

    leaving = []
    for q in range(4):
        columns = slice(q * step, (q + 1) * step)
        for j in range(2):
            ends = [factors[j, :, main:rows], factors[j, :, rows + main:]]
            total = jnp.dot(
                jnp.concatenate(ends, axis=1),
                jnp.concatenate([refs[j][main:, columns] for refs in tokens]),
                preferred_element_type=f32,
            )
            for t, refs in enumerate(tokens):
                total += jnp.dot(
                    factors[j, :, t * rows:t * rows + main], refs[j][:main, columns],
                    preferred_element_type=f32,
                )
            total = total.astype(bf16)
            for y in range(2):
                done[2 * q + y, j] = total[y * half:(y + 1) * half]
        block = pl.ds(2 * q, 2)
        leaving.append(pltpu.make_async_copy(done.at[block], out.at[block], go.at[q]))
        leaving[q].start()
    for copy in leaving:
        copy.wait()


def gradients(normed, normed_other, upstream, upstream_other, weights):
    units, step = weights.shape[1:]
    rows, width = normed.shape
    shape = (8, 2, units // 2, step)
    return pl.pallas_call(
        gradient_kernel,
        in_specs=[pl.BlockSpec(memory_space=pl.ANY)] * 5,
        out_specs=pl.BlockSpec(memory_space=pl.ANY),
        out_shape=jax.ShapeDtypeStruct(shape, bf16),
        scratch_shapes=[pltpu.VMEM((rows, width), bf16)] * 4
        + [
            pltpu.VMEM(weights.shape, bf16),
            pltpu.VMEM(shape, bf16),
            pltpu.VMEM((2, 2 * rows, units), f32),
            pltpu.VMEM((2, units, 2 * rows), bf16),
            pltpu.SemaphoreType.DMA((4, 5)),
            pltpu.SemaphoreType.DMA((4,)),
        ],
        compiler_params=pltpu.CompilerParams(vmem_limit_bytes=56 * MIB),
        name="gradients",
    )(normed, normed_other, upstream, upstream_other, weights)


def gather_z(block):
    depth = lax.axis_size("z")
    return lax.all_to_all(jnp.broadcast_to(block, (depth,) + block.shape), "z", 0, 0)


def gather_x(own):
    return shift(own, "x", 4, 1), shift(own, "x", 4, -1)


def gather_far(right, left):
    half = right.shape[0] // 2
    return shift(right[:half], "x", 4, 1), shift(left[half:], "x", 4, -1)


def on_device(
    token_ids, replica_table, embedding, ln_gain, ln_bias, weight_in, weight_out, cotangent
):
    replicas = replica_table.shape[0]
    tok = cotangent.shape[1]
    cols = cotangent.shape[2]
    half = tok // 2
    vocab_block = embedding.shape[0]
    units, width = weight_in.shape[1:]
    part = units // 2

    yh, core, x, yl = (lax.axis_index(a) for a in ("yh", "core", "x", "yl"))
    position = 2 * yh + core
    replica_index = jnp.arange(replicas, dtype=jnp.int32)
    source = jnp.min(jnp.where(replica_table[:, 1] == 1, replica_index, replicas))
    live_counts = tok * (4 + replica_table[:, 0]) // 6
    live = lax.dynamic_index_in_dim(live_counts, position, 0, keepdims=False)

    flag = (position == source).astype(jnp.int32).reshape(1)
    staged = stage(flag, weight_in[0], weight_out[0])
    share_w = lax.psum_scatter(
        staged.reshape(8 * units, width // 4), ("yh", "core"), scatter_dimension=0, tiled=True
    )

    cot = cotangent[0].reshape(2, 2, half // 2, cols)
    cot = jnp.concatenate([cot[:, 0], cot[:, 1]], axis=2)
    cot = jnp.broadcast_to(cot, (8,) + cot.shape).reshape((16,) + cot.shape[1:])

    vectors = jnp.concatenate([ln_gain.reshape(-1, 2 * cols), ln_bias.reshape(-1, 2 * cols)])
    share = vectors.shape[0] // 2
    held = jnp.concatenate([embedding.T, vectors], axis=1)
    ids = token_ids.reshape(4, 2, 2, 2, half // 2)
    ids = jnp.where(core == 0, ids[:, 0], ids[:, 1])
    local = jnp.bitwise_xor(ids - yh * 2 * vocab_block, core * vocab_block)
    low = local[:, :, 0].reshape(-1, 1)
    high = local[:, :, 1].reshape(-1, 1)

    info = jnp.stack([x, live, yl * half]).astype(jnp.int32)

    def slots(low, high, held, cot):
        cot = lax.all_to_all(cot, ("z", "yl"), 0, 0).reshape(8, half, 2 * cols)
        swapped = shift(held, "core", 2, 1)
        rows = lookup(low, high, held, swapped, vocab_block // 8).reshape(8, half // 2, 2 * cols)
        vectors = jnp.where(core == source % 2, held[:, vocab_block:], swapped[:, vocab_block:])
        vectors = lax.dynamic_slice_in_dim(vectors, yl * share, share, 0)
        sent = jnp.concatenate([rows, jnp.broadcast_to(vectors, (8,) + vectors.shape)], axis=1)
        sent, cot = lax.optimization_barrier((sent, cot))
        got = lax.all_to_all(sent, ("yh", "yl"), 0, 0)
        got, sides = lax.optimization_barrier((got, gather_x(cot)))
        far = gather_far(*sides)
        got = got.reshape((4, 2) + got.shape[1:])
        emb = jnp.sum(got[:, :, : half // 2].astype(f32), axis=0).astype(bf16)
        emb = emb.reshape(half, 2 * cols)
        root = lax.dynamic_index_in_dim(got[:, :, half // 2 :], source // 2, 0, keepdims=False)
        root = root.reshape(2, -1, 2 * cols).astype(f32)
        return (root[0], root[1], gather_z(emb), cot, *sides, *far)

    def no_slots(low, high, held, cot):
        lanes = 2 * cols
        vector, blocks = jnp.zeros((width // lanes, lanes), f32), jnp.zeros((8, half, lanes), bf16)
        return (vector, vector) + (blocks,) * 4 + (blocks[:4],) * 2

    def features(gain, bias, emb, *cot):
        upstream = assemble(merge_kernel, "merge", info, cot)
        sides, upstream = lax.optimization_barrier((gather_x(emb), upstream))
        blocks = (emb, *sides, *gather_far(*sides))
        normed = assemble(norm_kernel, "norm", info, blocks, (gain, bias))
        return normed, shift(normed, "core", 2, 1), upstream, shift(upstream, "core", 2, 1)

    def no_features(*blocks):
        return (jnp.zeros((half, width), bf16),) * 4

    some = source < replicas
    blocks = lax.cond(some, slots, no_slots, low, high, held, cot)
    *blocks, share_w = lax.optimization_barrier((*blocks, share_w))
    weights = lax.all_gather(share_w, ("yh", "yl"), tiled=True).reshape(8, units, width // 4)
    normed, normed_other, upstream, upstream_other = lax.cond(some, features, no_features, *blocks)
    terms = gradients(normed, normed_other, upstream, upstream_other, weights)
    terms = terms.reshape(16, part, width // 4)
    sums = lax.psum_scatter(terms, ("yh", "yl"), scatter_dimension=0, tiled=True)
    left, right = sums[:, :, : width // 8], sums[:, :, width // 8 :]
    theirs = shift(jnp.where(core == 0, right, left), "core", 2, 1)
    mine = jnp.where(core == 0, left, right)
    top = jnp.where(core == 0, mine, theirs)
    bottom = jnp.where(core == 0, theirs, mine)
    done = jnp.concatenate([top, bottom], axis=1)
    return done[0], done[1]


def solution(mesh):
    fine = Mesh(mesh.devices.reshape(4, 2, 8, 4, 2), ("yh", "core", "z", "x", "yl"))
    pipe, mp = ("yh", "core"), ("z", "x", "yl")
    placed = (
        P(),
        P(),
        P(pipe, mp),
        P(pipe, None),
        P(pipe, None),
        P(pipe, mp, None),
        P(pipe, mp, None),
        P(pipe, None, mp),
    )
    return jax.shard_map(
        on_device,
        mesh=fine,
        in_specs=placed,
        out_specs=(P(mp, pipe), P(mp, pipe)),
        check_vma=False,
    )
```

```python
import math

import jax
import jax.numpy as jnp
from jax import lax
from jax.experimental import pallas as pl
from jax.experimental.pallas import tpu as pltpu
from jax.sharding import Mesh, PartitionSpec as P

epsilon = 1e-05
bf16, f32 = jnp.bfloat16, jnp.float32
MIB = 1 << 20
SLOPE, CUBE = math.sqrt(2 / math.pi), 0.044715


def shift(value, axis, size, by):
    return lax.ppermute(value, axis, [(i, (i + by) % size) for i in range(size)])


def lookup_kernel(low_ref, high_ref, own_ref, other_ref, out_ref, groups):
    width = own_ref.shape[0]
    count, depth = 8, groups.shape[1]

    @pl.when(pl.program_id(0) == 0)
    def _():
        for b, ref in enumerate((own_ref, other_ref)):
            for k in range(count):
                base = (b * count + k) * width
                groups[base:base + width, :] = ref[:, k * depth:(k + 1) * depth]

    rows = out_ref.shape[0]
    place = lax.broadcasted_iota(jnp.int32, (rows, depth), 1)
    lane = lax.broadcasted_iota(jnp.int32, (rows, 2 * width), 1)
    total = jnp.zeros((rows, 2 * width), f32)
    for side, ref in enumerate((low_ref, high_ref)):
        ids = ref[...]
        group = jnp.right_shift(ids, 9)
        inner = jnp.bitwise_and(ids, depth - 1)
        hot = (place == inner).astype(f32).astype(bf16)
        picked = lax.dot_general(
            hot, groups[...], (((1,), (1,)), ((), ())), preferred_element_type=f32
        )
        pair = jnp.right_shift(group, 1)
        found = jnp.zeros((rows, 2 * width), f32)
        for j in range(count):
            found += jnp.where(pair == j, picked[:, 2 * j * width:2 * (j + 1) * width], 0.0)
        turned = pltpu.roll(found, width, 1)
        found = jnp.where(jnp.bitwise_and(group, 1) == side, found, turned)
        total += jnp.where((lane >= width) == (side == 1), found, 0.0)
    out_ref[...] = total.astype(bf16)


def lookup(low, high, own, other, depth):
    rows = low.shape[0]
    width, lanes = own.shape
    step = rows // 2
    return pl.pallas_call(
        lookup_kernel,
        grid=(2,),
        in_specs=[
            pl.BlockSpec((step, 1), lambda i: (i, 0)),
            pl.BlockSpec((step, 1), lambda i: (i, 0)),
            pl.BlockSpec((width, lanes), lambda i: (0, 0)),
            pl.BlockSpec((width, lanes), lambda i: (0, 0)),
        ],
        out_specs=pl.BlockSpec((step, 2 * width), lambda i: (i, 0)),
        out_shape=jax.ShapeDtypeStruct((rows, 2 * width), bf16),
        scratch_shapes=[pltpu.VMEM((16 * width, depth), bf16)],
        compiler_params=pltpu.CompilerParams(vmem_limit_bytes=32 * MIB),
        name="lookup",
    )(low, high, own, other)


def laid_out(info_ref, blocks):
    x = info_ref[0]
    own, right, left, far0, far1 = blocks
    depth, rows, lanes = own.shape
    half = depth // 2
    for k in range(depth):
        far = far0.at[k] if k < half else far1.at[k - half]
        for by, ref in ((0, own.at[k]), (3, right.at[k]), (1, left.at[k]), (2, far)):
            spot = 4 * k + jnp.bitwise_and(x + by, 3)
            yield ref, spot, pl.ds(pl.multiple_of(spot * lanes, lanes), lanes)


def unpacked(ref, start, step):
    rows, lanes = ref.shape
    half = lanes // 2
    first = ref[pl.ds(start, step), :].astype(f32)
    second = ref[pl.ds(rows // 2 + start, step), :].astype(f32)
    low = lax.broadcasted_iota(jnp.int32, (step, lanes), 1) < half
    return (
        jnp.where(low, first, pltpu.roll(second, half, 1)),
        jnp.where(low, pltpu.roll(first, half, 1), second),
    )


STEP = 48


def merge_kernel(info_ref, *refs):
    *blocks, out_ref = refs
    live, first = info_ref[1], info_ref[2]
    _, rows, lanes = blocks[0].shape

    @pl.loop(0, rows // 2 // STEP)
    def _(i):
        start = pl.multiple_of(i * STEP, STEP)
        slot = lax.broadcasted_iota(jnp.int32, (STEP, lanes), 0) + first + start
        for ref, _, here in laid_out(info_ref, blocks):
            for side, v in enumerate(unpacked(ref, start, STEP)):
                base = side * (rows // 2)
                v = jnp.where(slot + base < live, v, 0.0)
                out_ref[pl.ds(pl.multiple_of(base + start, STEP), STEP), here] = v.astype(bf16)


def norm_kernel(info_ref, *refs):
    *blocks, gain_ref, bias_ref, out_ref = refs
    _, rows, lanes = blocks[0].shape
    full = out_ref.shape[1]

    @pl.loop(0, rows // 2 // STEP)
    def _(i):
        start = pl.multiple_of(i * STEP, STEP)
        here = [pl.ds(pl.multiple_of(start + s * (rows // 2), STEP), STEP) for s in range(2)]
        zeros = jnp.zeros((STEP, lanes), f32)
        total, square = [zeros, zeros], [zeros, zeros]
        for ref, _, columns in laid_out(info_ref, blocks):
            for side, v in enumerate(unpacked(ref, start, STEP)):
                total[side] += v
                square[side] += v * v
                out_ref[here[side], columns] = v.astype(bf16)
        for side in range(2):
            mean = jnp.sum(total[side], axis=1, keepdims=True) / full
            power = jnp.sum(square[side], axis=1, keepdims=True) / full
            scale = lax.rsqrt(power - mean * mean + epsilon)
            for k in range(full // lanes):
                columns = slice(k * lanes, (k + 1) * lanes)
                v = (out_ref[here[side], columns].astype(f32) - mean) * scale
                v = v * gain_ref[k:k + 1, :] + bias_ref[k:k + 1, :]
                out_ref[here[side], columns] = v.astype(bf16)


def assemble(kernel, name, info, blocks, extra=()):
    depth, rows, lanes = blocks[0].shape
    return pl.pallas_call(
        kernel,
        in_specs=[pl.BlockSpec(memory_space=pltpu.SMEM)]
        + [pl.BlockSpec(memory_space=pltpu.VMEM)] * (len(blocks) + len(extra)),
        out_specs=pl.BlockSpec(memory_space=pltpu.VMEM),
        out_shape=jax.ShapeDtypeStruct((rows, 4 * depth * lanes), bf16),
        compiler_params=pltpu.CompilerParams(vmem_limit_bytes=32 * MIB),
        name=name,
    )(info, *blocks, *extra)


def gradient_kernel(
    normed0, normed1, up0, up1, weights, out, rows0, rows1, rows2, rows3, held, done, acc, factors,
    come, go,
):
    units, width = weights.shape[1:]
    step = width // 4
    rows = normed0.shape[0]
    tokens = ((rows0, rows2), (rows1, rows3))
    half = units // 2
    main = 256

    copies = []
    for k in range(4):
        columns = pl.ds(k * step, step)
        pairs = [(weights.at[:, :, columns], held.at[:, :, columns])]
        for source, target in ((normed0, rows0), (normed1, rows1), (up0, rows2), (up1, rows3)):
            pairs.append((source.at[:, columns], target.at[:, columns]))
        copies.append(
            [pltpu.make_async_copy(a, b, come.at[k, n]) for n, (a, b) in enumerate(pairs)]
        )
        for copy in copies[k]:
            copy.start()

    for k in range(4):
        for copy in copies[k]:
            copy.wait()
        for j in range(2):
            for t, refs in enumerate(tokens):
                here = (j, slice(t * rows, (t + 1) * rows))
                term = lax.dot_general(
                    refs[j][:, k * step:(k + 1) * step], held[j, :, k * step:(k + 1) * step],
                    (((1,), (1,)), ((), ())), preferred_element_type=f32,
                )
                acc[here] = term if k == 0 else acc[here] + term

    value = acc[0]
    bent = jnp.tanh(SLOPE * (value + CUBE * value * value * value))
    slope = 0.5 * (1.0 + bent) + 0.5 * value * (1.0 - bent * bent) * (
        SLOPE * (1.0 + 3.0 * CUBE * value * value)
    )
    factors[0] = jnp.transpose(acc[1] * slope).astype(bf16)
    factors[1] = jnp.transpose(0.5 * value * (1.0 + bent)).astype(bf16)

    leaving = []
    for q in range(4):
        columns = slice(q * step, (q + 1) * step)
        for j in range(2):
            ends = [factors[j, :, main:rows], factors[j, :, rows + main:]]
            total = jnp.dot(
                jnp.concatenate(ends, axis=1),
                jnp.concatenate([refs[j][main:, columns] for refs in tokens]),
                preferred_element_type=f32,
            )
            for t, refs in enumerate(tokens):
                total += jnp.dot(
                    factors[j, :, t * rows:t * rows + main], refs[j][:main, columns],
                    preferred_element_type=f32,
                )
            total = total.astype(bf16)
            for y in range(2):
                done[2 * q + y, j] = total[y * half:(y + 1) * half]
        block = pl.ds(2 * q, 2)
        leaving.append(pltpu.make_async_copy(done.at[block], out.at[block], go.at[q]))
        leaving[q].start()
    for copy in leaving:
        copy.wait()


def gradients(normed, normed_other, upstream, upstream_other, weights):
    units, width = weights.shape[1:]
    rows, step = normed.shape[0], width // 4
    shape = (8, 2, units // 2, step)
    return pl.pallas_call(
        gradient_kernel,
        in_specs=[pl.BlockSpec(memory_space=pl.ANY)] * 5,
        out_specs=pl.BlockSpec(memory_space=pl.ANY),
        out_shape=jax.ShapeDtypeStruct(shape, bf16),
        scratch_shapes=[pltpu.VMEM((rows, width), bf16)] * 4
        + [
            pltpu.VMEM(weights.shape, bf16),
            pltpu.VMEM(shape, bf16),
            pltpu.VMEM((2, 2 * rows, units), f32),
            pltpu.VMEM((2, units, 2 * rows), bf16),
            pltpu.SemaphoreType.DMA((4, 5)),
            pltpu.SemaphoreType.DMA((4,)),
        ],
        compiler_params=pltpu.CompilerParams(vmem_limit_bytes=56 * MIB),
        name="gradients",
    )(normed, normed_other, upstream, upstream_other, weights)


def gather_z(block):
    depth = lax.axis_size("z")
    return lax.all_to_all(jnp.broadcast_to(block, (depth,) + block.shape), "z", 0, 0)


def gather_x(own):
    return shift(own, "x", 4, 1), shift(own, "x", 4, -1)


def gather_far(right, left):
    half = right.shape[0] // 2
    return shift(right[:half], "x", 4, 1), shift(left[half:], "x", 4, -1)


def on_device(
    token_ids, replica_table, embedding, ln_gain, ln_bias, weight_in, weight_out, cotangent
):
    replicas = replica_table.shape[0]
    tok = cotangent.shape[1]
    cols = cotangent.shape[2]
    half = tok // 2
    vocab_block = embedding.shape[0]
    units, width = weight_in.shape[1:]
    part = units // 2

    yh, core, x, yl = (lax.axis_index(a) for a in ("yh", "core", "x", "yl"))
    position = 2 * yh + core
    replica_index = jnp.arange(replicas, dtype=jnp.int32)
    source = jnp.min(jnp.where(replica_table[:, 1] == 1, replica_index, replicas))
    live_counts = tok * (4 + replica_table[:, 0]) // 6
    live = lax.dynamic_index_in_dim(live_counts, position, 0, keepdims=False)

    pair = jnp.stack([weight_in[0], weight_out[0]]).reshape(2, 2, part, width)
    theirs = jnp.where(core == 0, pair[:, 1], pair[:, 0])
    mine = jnp.where(core == 0, pair[:, 0], pair[:, 1])
    mine = jnp.where(core == source % 2, mine, shift(theirs, "core", 2, 1))
    slot = jnp.arange(2).reshape(1, 2, 1, 1)
    spread = jnp.where((slot == yl) & (yh == source // 2), mine[:, None], jnp.zeros((), bf16))
    spread = spread.reshape(2, 2 * part, width)

    cot = cotangent[0].reshape(2, 2, half // 2, cols)
    cot = jnp.concatenate([cot[:, 0], cot[:, 1]], axis=2)
    cot = lax.all_to_all(cot, "yl", 0, 0).reshape(half, 2 * cols)
    spread, cot = lax.optimization_barrier((spread, cot))

    vectors = jnp.concatenate([ln_gain.reshape(-1, 2 * cols), ln_bias.reshape(-1, 2 * cols)])
    share = vectors.shape[0] // 2
    vectors = lax.dynamic_slice_in_dim(vectors, yl * share, share, 0)
    table = embedding.T
    ids = token_ids.reshape(4, 2, 2, 2, half // 2)
    ids = jnp.where(core == 0, ids[:, 0], ids[:, 1])
    local = jnp.bitwise_xor(ids - yh * 2 * vocab_block, core * vocab_block)
    low = local[:, :, 0].reshape(-1, 1)
    high = local[:, :, 1].reshape(-1, 1)
    weights = lax.psum(spread, ("yh", "yl"))

    def slots(low, high, table, vectors, cot):
        cot = gather_z(cot)
        swapped = shift(table, "core", 2, 1)
        rows = lookup(low, high, table, swapped, vocab_block // 8).reshape(8, half // 2, 2 * cols)
        sent = jnp.concatenate([rows, jnp.broadcast_to(vectors, (8,) + vectors.shape)], axis=1)
        sent, cot = lax.optimization_barrier((sent, cot))
        got = lax.all_to_all(sent, ("yh", "yl"), 0, 0)
        info = jnp.stack([x, live, yl * half]).astype(jnp.int32)
        got, sides = lax.optimization_barrier((got, gather_x(cot)))
        far = gather_far(*sides)
        got = got.reshape((4, 2) + got.shape[1:])
        emb = jnp.sum(got[:, :, : half // 2].astype(f32), axis=0).astype(bf16)
        emb = emb.reshape(half, 2 * cols)
        root = lax.dynamic_index_in_dim(got[:, :, half // 2 :], source // 2, 0, keepdims=False)
        root = jnp.where(core == source % 2, root, shift(root, "core", 2, 1))
        root = root.reshape(2, -1, 2 * cols).astype(f32)
        emb, far = lax.optimization_barrier((gather_z(emb), far))
        upstream = assemble(merge_kernel, "merge", info, (cot, *sides, *far))
        sides, upstream = lax.optimization_barrier((gather_x(emb), upstream))
        blocks = (emb, *sides, *gather_far(*sides))
        normed = assemble(norm_kernel, "norm", info, blocks, (root[0], root[1]))
        return normed, shift(normed, "core", 2, 1), upstream, shift(upstream, "core", 2, 1)

    def nothing(low, high, table, vectors, cot):
        return (jnp.zeros((half, width), bf16),) * 4

    normed, normed_other, upstream, upstream_other = lax.cond(
        source < replicas, slots, nothing, low, high, table, vectors, cot
    )
    terms = gradients(normed, normed_other, upstream, upstream_other, weights)
    terms = terms.reshape(16, part, width // 4)
    sums = lax.psum_scatter(terms, ("yh", "yl"), scatter_dimension=0, tiled=True)
    left, right = sums[:, :, : width // 8], sums[:, :, width // 8 :]
    theirs = shift(jnp.where(core == 0, right, left), "core", 2, 1)
    mine = jnp.where(core == 0, left, right)
    top = jnp.where(core == 0, mine, theirs)
    bottom = jnp.where(core == 0, theirs, mine)
    done = jnp.concatenate([top, bottom], axis=1)
    return done[0], done[1]


def solution(mesh):
    fine = Mesh(mesh.devices.reshape(4, 2, 8, 4, 2), ("yh", "core", "z", "x", "yl"))
    pipe, mp = ("yh", "core"), ("z", "x", "yl")
    placed = (
        P(),
        P(),
        P(pipe, mp),
        P(pipe, None),
        P(pipe, None),
        P(pipe, mp, None),
        P(pipe, mp, None),
        P(pipe, None, mp),
    )
    return jax.shard_map(
        on_device,
        mesh=fine,
        in_specs=placed,
        out_specs=(P(mp, pipe), P(mp, pipe)),
        check_vma=False,
    )
```

```python
import math

import jax
import jax.numpy as jnp
from jax import lax
from jax.experimental import pallas as pl
from jax.experimental.pallas import tpu as pltpu
from jax.sharding import Mesh, PartitionSpec as P

epsilon = 1e-05
bf16, f32 = jnp.bfloat16, jnp.float32
MIB = 1 << 20
SLOPE, CUBE = math.sqrt(2 / math.pi), 0.044715


def shift(value, axis, size, by):
    return lax.ppermute(value, axis, [(i, (i + by) % size) for i in range(size)])


def lookup_kernel(low_ref, high_ref, own_ref, other_ref, out_ref, groups):
    width = own_ref.shape[0]
    count, depth = 8, groups.shape[1]

    @pl.when(pl.program_id(0) == 0)
    def _():
        for b, ref in enumerate((own_ref, other_ref)):
            for k in range(count):
                base = (b * count + k) * width
                groups[base:base + width, :] = ref[:, k * depth:(k + 1) * depth]

    rows = out_ref.shape[0]
    place = lax.broadcasted_iota(jnp.int32, (rows, depth), 1)
    lane = lax.broadcasted_iota(jnp.int32, (rows, 2 * width), 1)
    total = jnp.zeros((rows, 2 * width), f32)
    for side, ref in enumerate((low_ref, high_ref)):
        ids = ref[...]
        group = jnp.right_shift(ids, 9)
        inner = jnp.bitwise_and(ids, depth - 1)
        hot = (place == inner).astype(f32).astype(bf16)
        picked = lax.dot_general(
            hot, groups[...], (((1,), (1,)), ((), ())), preferred_element_type=f32
        )
        pair = jnp.right_shift(group, 1)
        found = jnp.zeros((rows, 2 * width), f32)
        for j in range(count):
            found += jnp.where(pair == j, picked[:, 2 * j * width:2 * (j + 1) * width], 0.0)
        turned = pltpu.roll(found, width, 1)
        found = jnp.where(jnp.bitwise_and(group, 1) == side, found, turned)
        total += jnp.where((lane >= width) == (side == 1), found, 0.0)
    out_ref[...] = total.astype(bf16)


def lookup(low, high, own, other, depth):
    rows = low.shape[0]
    width, lanes = own.shape
    step = rows // 2
    return pl.pallas_call(
        lookup_kernel,
        grid=(2,),
        in_specs=[
            pl.BlockSpec((step, 1), lambda i: (i, 0)),
            pl.BlockSpec((step, 1), lambda i: (i, 0)),
            pl.BlockSpec((width, lanes), lambda i: (0, 0)),
            pl.BlockSpec((width, lanes), lambda i: (0, 0)),
        ],
        out_specs=pl.BlockSpec((step, 2 * width), lambda i: (i, 0)),
        out_shape=jax.ShapeDtypeStruct((rows, 2 * width), bf16),
        scratch_shapes=[pltpu.VMEM((16 * width, depth), bf16)],
        compiler_params=pltpu.CompilerParams(vmem_limit_bytes=32 * MIB),
        name="lookup",
    )(low, high, own, other)


def laid_out(info_ref, blocks):
    x = info_ref[0]
    own, right, left, far0, far1 = blocks
    depth, rows, lanes = own.shape
    half = depth // 2
    for k in range(depth):
        far = far0.at[k] if k < half else far1.at[k - half]
        for by, ref in ((0, own.at[k]), (3, right.at[k]), (1, left.at[k]), (2, far)):
            spot = 4 * k + jnp.bitwise_and(x + by, 3)
            yield ref, spot, pl.ds(pl.multiple_of(spot * lanes, lanes), lanes)


def unpacked(ref, start, step):
    rows, lanes = ref.shape
    half = lanes // 2
    first = ref[pl.ds(start, step), :].astype(f32)
    second = ref[pl.ds(rows // 2 + start, step), :].astype(f32)
    low = lax.broadcasted_iota(jnp.int32, (step, lanes), 1) < half
    return (
        jnp.where(low, first, pltpu.roll(second, half, 1)),
        jnp.where(low, pltpu.roll(first, half, 1), second),
    )


STEP = 48


def merge_kernel(info_ref, *refs):
    *blocks, out_ref = refs
    live, first = info_ref[1], info_ref[2]
    _, rows, lanes = blocks[0].shape

    @pl.loop(0, rows // 2 // STEP)
    def _(i):
        start = pl.multiple_of(i * STEP, STEP)
        slot = lax.broadcasted_iota(jnp.int32, (STEP, lanes), 0) + first + start
        for ref, _, here in laid_out(info_ref, blocks):
            for side, v in enumerate(unpacked(ref, start, STEP)):
                base = side * (rows // 2)
                v = jnp.where(slot + base < live, v, 0.0)
                out_ref[pl.ds(pl.multiple_of(base + start, STEP), STEP), here] = v.astype(bf16)


def norm_kernel(info_ref, *refs):
    *blocks, gain_ref, bias_ref, out_ref = refs
    _, rows, lanes = blocks[0].shape
    full = out_ref.shape[1]

    @pl.loop(0, rows // 2 // STEP)
    def _(i):
        start = pl.multiple_of(i * STEP, STEP)
        here = [pl.ds(pl.multiple_of(start + s * (rows // 2), STEP), STEP) for s in range(2)]
        zeros = jnp.zeros((STEP, lanes), f32)
        total, square = [zeros, zeros], [zeros, zeros]
        for ref, _, columns in laid_out(info_ref, blocks):
            for side, v in enumerate(unpacked(ref, start, STEP)):
                total[side] += v
                square[side] += v * v
                out_ref[here[side], columns] = v.astype(bf16)
        for side in range(2):
            mean = jnp.sum(total[side], axis=1, keepdims=True) / full
            power = jnp.sum(square[side], axis=1, keepdims=True) / full
            scale = lax.rsqrt(power - mean * mean + epsilon)
            for k in range(full // lanes):
                columns = slice(k * lanes, (k + 1) * lanes)
                v = (out_ref[here[side], columns].astype(f32) - mean) * scale
                v = v * gain_ref[k:k + 1, :] + bias_ref[k:k + 1, :]
                out_ref[here[side], columns] = v.astype(bf16)


def assemble(kernel, name, info, blocks, extra=()):
    depth, rows, lanes = blocks[0].shape
    return pl.pallas_call(
        kernel,
        in_specs=[pl.BlockSpec(memory_space=pltpu.SMEM)]
        + [pl.BlockSpec(memory_space=pltpu.VMEM)] * (len(blocks) + len(extra)),
        out_specs=pl.BlockSpec(memory_space=pltpu.VMEM),
        out_shape=jax.ShapeDtypeStruct((rows, 4 * depth * lanes), bf16),
        compiler_params=pltpu.CompilerParams(vmem_limit_bytes=32 * MIB),
        name=name,
    )(info, *blocks, *extra)


def stage_kernel(flag_ref, first, second, out, come, leave, come_sem, leave_sem):
    units, width = first.shape
    half, step = units // 2, width // 4
    copies = []
    for k in range(4):
        columns = pl.ds(k * step, step)
        for j, source in enumerate((first, second)):
            copies.append(
                pltpu.make_async_copy(source.at[:, columns], come.at[k, j], come_sem.at[k, j])
            )
            copies[-1].start()
    leaving = []
    for k in range(4):
        for j in range(2):
            copies[2 * k + j].wait()
            for c in range(2):
                kept = come[k, j, c * half:(c + 1) * half, :].astype(f32)
                kept = jnp.where(flag_ref[0] == 1, kept, 0.0)
                leave[2 * k + c, j * half:(j + 1) * half, :] = kept.astype(bf16)
        block = pl.ds(2 * k, 2)
        leaving.append(pltpu.make_async_copy(leave.at[block], out.at[block], leave_sem.at[k]))
        leaving[k].start()
    for copy in leaving:
        copy.wait()


def stage(flag, first, second):
    units, width = first.shape
    return pl.pallas_call(
        stage_kernel,
        in_specs=[pl.BlockSpec(memory_space=pltpu.SMEM)] + [pl.BlockSpec(memory_space=pl.ANY)] * 2,
        out_specs=pl.BlockSpec(memory_space=pl.ANY),
        out_shape=jax.ShapeDtypeStruct((8, units, width // 4), bf16),
        scratch_shapes=[
            pltpu.VMEM((4, 2, units, width // 4), bf16),
            pltpu.VMEM((8, units, width // 4), bf16),
            pltpu.SemaphoreType.DMA((4, 2)),
            pltpu.SemaphoreType.DMA((4,)),
        ],
        compiler_params=pltpu.CompilerParams(vmem_limit_bytes=60 * MIB),
        name="stage",
    )(flag, first, second)


def gradient_kernel(
    normed0, normed1, up0, up1, weights, out, rows0, rows1, rows2, rows3, held, done, acc, factors,
    come, go,
):
    units, step = weights.shape[1:]
    rows = normed0.shape[0]
    tokens = ((rows0, rows2), (rows1, rows3))
    half = units // 2
    main = 256

    copies = []
    for k in range(4):
        columns = pl.ds(k * step, step)
        pairs = [(weights.at[pl.ds(2 * k, 2)], held.at[pl.ds(2 * k, 2)])]
        for source, target in ((normed0, rows0), (normed1, rows1), (up0, rows2), (up1, rows3)):
            pairs.append((source.at[:, columns], target.at[:, columns]))
        copies.append(
            [pltpu.make_async_copy(a, b, come.at[k, n]) for n, (a, b) in enumerate(pairs)]
        )
        for copy in copies[k]:
            copy.start()

    for k in range(4):
        for copy in copies[k]:
            copy.wait()
        for j in range(2):
            both = jnp.concatenate(
                [held[2 * k + y, j * half:(j + 1) * half, :] for y in range(2)]
            )
            for t, refs in enumerate(tokens):
                here = (j, slice(t * rows, (t + 1) * rows))
                term = lax.dot_general(
                    refs[j][:, k * step:(k + 1) * step], both, (((1,), (1,)), ((), ())),
                    preferred_element_type=f32,
                )
                acc[here] = term if k == 0 else acc[here] + term

    value = acc[0]
    bent = jnp.tanh(SLOPE * (value + CUBE * value * value * value))
    slope = 0.5 * (1.0 + bent) + 0.5 * value * (1.0 - bent * bent) * (
        SLOPE * (1.0 + 3.0 * CUBE * value * value)
    )
    factors[0] = jnp.transpose(acc[1] * slope).astype(bf16)
    factors[1] = jnp.transpose(0.5 * value * (1.0 + bent)).astype(bf16)

    leaving = []
    for q in range(4):
        columns = slice(q * step, (q + 1) * step)
        for j in range(2):
            ends = [factors[j, :, main:rows], factors[j, :, rows + main:]]
            total = jnp.dot(
                jnp.concatenate(ends, axis=1),
                jnp.concatenate([refs[j][main:, columns] for refs in tokens]),
                preferred_element_type=f32,
            )
            for t, refs in enumerate(tokens):
                total += jnp.dot(
                    factors[j, :, t * rows:t * rows + main], refs[j][:main, columns],
                    preferred_element_type=f32,
                )
            total = total.astype(bf16)
            for y in range(2):
                done[2 * q + y, j] = total[y * half:(y + 1) * half]
        block = pl.ds(2 * q, 2)
        leaving.append(pltpu.make_async_copy(done.at[block], out.at[block], go.at[q]))
        leaving[q].start()
    for copy in leaving:
        copy.wait()


def gradients(normed, normed_other, upstream, upstream_other, weights):
    units, step = weights.shape[1:]
    rows, width = normed.shape
    shape = (8, 2, units // 2, step)
    return pl.pallas_call(
        gradient_kernel,
        in_specs=[pl.BlockSpec(memory_space=pl.ANY)] * 5,
        out_specs=pl.BlockSpec(memory_space=pl.ANY),
        out_shape=jax.ShapeDtypeStruct(shape, bf16),
        scratch_shapes=[pltpu.VMEM((rows, width), bf16)] * 4
        + [
            pltpu.VMEM(weights.shape, bf16),
            pltpu.VMEM(shape, bf16),
            pltpu.VMEM((2, 2 * rows, units), f32),
            pltpu.VMEM((2, units, 2 * rows), bf16),
            pltpu.SemaphoreType.DMA((4, 5)),
            pltpu.SemaphoreType.DMA((4,)),
        ],
        compiler_params=pltpu.CompilerParams(vmem_limit_bytes=56 * MIB),
        name="gradients",
    )(normed, normed_other, upstream, upstream_other, weights)


def gather_z(block):
    depth = lax.axis_size("z")
    return lax.all_to_all(jnp.broadcast_to(block, (depth,) + block.shape), "z", 0, 0)


def gather_x(own):
    return shift(own, "x", 4, 1), shift(own, "x", 4, -1)


def gather_far(right, left):
    half = right.shape[0] // 2
    return shift(right[:half], "x", 4, 1), shift(left[half:], "x", 4, -1)


def on_device(
    token_ids, replica_table, embedding, ln_gain, ln_bias, weight_in, weight_out, cotangent
):
    replicas = replica_table.shape[0]
    tok = cotangent.shape[1]
    cols = cotangent.shape[2]
    half = tok // 2
    vocab_block = embedding.shape[0]
    units, width = weight_in.shape[1:]
    part = units // 2

    yh, core, x, yl = (lax.axis_index(a) for a in ("yh", "core", "x", "yl"))
    position = 2 * yh + core
    replica_index = jnp.arange(replicas, dtype=jnp.int32)
    source = jnp.min(jnp.where(replica_table[:, 1] == 1, replica_index, replicas))
    live_counts = tok * (4 + replica_table[:, 0]) // 6
    live = lax.dynamic_index_in_dim(live_counts, position, 0, keepdims=False)

    flag = (position == source).astype(jnp.int32).reshape(1)
    staged = stage(flag, weight_in[0], weight_out[0])
    share_w = lax.psum_scatter(
        staged.reshape(8 * units, width // 4), ("yh", "core"), scatter_dimension=0, tiled=True
    )

    cot = cotangent[0].reshape(2, 2, half // 2, cols)
    cot = jnp.concatenate([cot[:, 0], cot[:, 1]], axis=2)
    cot = jnp.broadcast_to(cot, (8,) + cot.shape).reshape((16,) + cot.shape[1:])

    vectors = jnp.concatenate([ln_gain.reshape(-1, 2 * cols), ln_bias.reshape(-1, 2 * cols)])
    share = vectors.shape[0] // 2
    held = jnp.concatenate([embedding.T, vectors], axis=1)
    ids = token_ids.reshape(4, 2, 2, 2, half // 2)
    ids = jnp.where(core == 0, ids[:, 0], ids[:, 1])
    local = jnp.bitwise_xor(ids - yh * 2 * vocab_block, core * vocab_block)
    low = local[:, :, 0].reshape(-1, 1)
    high = local[:, :, 1].reshape(-1, 1)

    info = jnp.stack([x, live, yl * half]).astype(jnp.int32)

    def slots(low, high, held, cot):
        cot = lax.all_to_all(cot, ("z", "yl"), 0, 0).reshape(8, half, 2 * cols)
        swapped = shift(held, "core", 2, 1)
        rows = lookup(low, high, held, swapped, vocab_block // 8).reshape(8, half // 2, 2 * cols)
        vectors = jnp.where(core == source % 2, held[:, vocab_block:], swapped[:, vocab_block:])
        vectors = lax.dynamic_slice_in_dim(vectors, yl * share, share, 0)
        sent = jnp.concatenate([rows, jnp.broadcast_to(vectors, (8,) + vectors.shape)], axis=1)
        sent, cot = lax.optimization_barrier((sent, cot))
        got = lax.all_to_all(sent, ("yh", "yl"), 0, 0)
        got, sides = lax.optimization_barrier((got, gather_x(cot)))
        far = gather_far(*sides)
        got = got.reshape((4, 2) + got.shape[1:])
        emb = jnp.sum(got[:, :, : half // 2].astype(f32), axis=0).astype(bf16)
        emb = emb.reshape(half, 2 * cols)
        root = lax.dynamic_index_in_dim(got[:, :, half // 2 :], source // 2, 0, keepdims=False)
        root = root.reshape(2, -1, 2 * cols).astype(f32)
        return (root[0], root[1], gather_z(emb), cot, *sides, *far)

    def no_slots(low, high, held, cot):
        lanes = 2 * cols
        vector, blocks = jnp.zeros((width // lanes, lanes), f32), jnp.zeros((8, half, lanes), bf16)
        return (vector, vector) + (blocks,) * 4 + (blocks[:4],) * 2

    def features(gain, bias, emb, *cot):
        upstream = assemble(merge_kernel, "merge", info, cot)
        sides, upstream = lax.optimization_barrier((gather_x(emb), upstream))
        blocks = (emb, *sides, *gather_far(*sides))
        normed = assemble(norm_kernel, "norm", info, blocks, (gain, bias))
        return normed, shift(normed, "core", 2, 1), upstream, shift(upstream, "core", 2, 1)

    def no_features(*blocks):
        return (jnp.zeros((half, width), bf16),) * 4

    some = source < replicas
    blocks = lax.cond(some, slots, no_slots, low, high, held, cot)
    *blocks, share_w = lax.optimization_barrier((*blocks, share_w))
    weights = lax.all_gather(share_w, ("yh", "yl"), tiled=True).reshape(8, units, width // 4)
    normed, normed_other, upstream, upstream_other = lax.cond(some, features, no_features, *blocks)
    terms = gradients(normed, normed_other, upstream, upstream_other, weights)
    terms = terms.reshape(16, part, width // 4)
    sums = lax.psum_scatter(terms, ("yh", "yl"), scatter_dimension=0, tiled=True)
    left, right = sums[:, :, : width // 8], sums[:, :, width // 8 :]
    theirs = shift(jnp.where(core == 0, right, left), "core", 2, 1)
    mine = jnp.where(core == 0, left, right)
    top = jnp.where(core == 0, mine, theirs)
    bottom = jnp.where(core == 0, theirs, mine)
    done = jnp.concatenate([top, bottom], axis=1)
    return done[0], done[1]


def solution(mesh):
    fine = Mesh(mesh.devices.reshape(4, 2, 8, 4, 2), ("yh", "core", "z", "x", "yl"))
    pipe, mp = ("yh", "core"), ("z", "x", "yl")
    placed = (
        P(),
        P(),
        P(pipe, mp),
        P(pipe, None),
        P(pipe, None),
        P(pipe, mp, None),
        P(pipe, mp, None),
        P(pipe, None, mp),
    )
    return jax.shard_map(
        on_device,
        mesh=fine,
        in_specs=placed,
        out_specs=(P(mp, pipe), P(mp, pipe)),
        check_vma=False,
    )
```

```python
import math

import jax
import jax.numpy as jnp
from jax import lax
from jax.experimental import pallas as pl
from jax.experimental.pallas import tpu as pltpu
from jax.sharding import Mesh, PartitionSpec as P

epsilon = 1e-05
bf16, f32 = jnp.bfloat16, jnp.float32
MIB = 1 << 20
SLOPE, CUBE = math.sqrt(2 / math.pi), 0.044715


def shift(value, axis, size, by):
    return lax.ppermute(value, axis, [(i, (i + by) % size) for i in range(size)])


def lookup_kernel(low_ref, high_ref, own_ref, other_ref, out_ref, groups):
    width = own_ref.shape[0]
    count, depth = 8, groups.shape[1]

    @pl.when(pl.program_id(0) == 0)
    def _():
        for b, ref in enumerate((own_ref, other_ref)):
            for k in range(count):
                base = (b * count + k) * width
                groups[base:base + width, :] = ref[:, k * depth:(k + 1) * depth]

    rows = out_ref.shape[0]
    place = lax.broadcasted_iota(jnp.int32, (rows, depth), 1)
    lane = lax.broadcasted_iota(jnp.int32, (rows, 2 * width), 1)
    total = jnp.zeros((rows, 2 * width), f32)
    for side, ref in enumerate((low_ref, high_ref)):
        ids = ref[...]
        group = jnp.right_shift(ids, 9)
        inner = jnp.bitwise_and(ids, depth - 1)
        hot = (place == inner).astype(f32).astype(bf16)
        picked = lax.dot_general(
            hot, groups[...], (((1,), (1,)), ((), ())), preferred_element_type=f32
        )
        pair = jnp.right_shift(group, 1)
        found = jnp.zeros((rows, 2 * width), f32)
        for j in range(count):
            found += jnp.where(pair == j, picked[:, 2 * j * width:2 * (j + 1) * width], 0.0)
        turned = pltpu.roll(found, width, 1)
        found = jnp.where(jnp.bitwise_and(group, 1) == side, found, turned)
        total += jnp.where((lane >= width) == (side == 1), found, 0.0)
    out_ref[...] = total.astype(bf16)


def lookup(low, high, own, other, depth):
    rows = low.shape[0]
    width, lanes = own.shape
    step = rows // 2
    return pl.pallas_call(
        lookup_kernel,
        grid=(2,),
        in_specs=[
            pl.BlockSpec((step, 1), lambda i: (i, 0)),
            pl.BlockSpec((step, 1), lambda i: (i, 0)),
            pl.BlockSpec((width, lanes), lambda i: (0, 0)),
            pl.BlockSpec((width, lanes), lambda i: (0, 0)),
        ],
        out_specs=pl.BlockSpec((step, 2 * width), lambda i: (i, 0)),
        out_shape=jax.ShapeDtypeStruct((rows, 2 * width), bf16),
        scratch_shapes=[pltpu.VMEM((16 * width, depth), bf16)],
        compiler_params=pltpu.CompilerParams(vmem_limit_bytes=32 * MIB),
        name="lookup",
    )(low, high, own, other)


def laid_out(info_ref, blocks):
    x = info_ref[0]
    own, right, left, far0, far1 = blocks
    depth, rows, lanes = own.shape
    half = depth // 2
    for k in range(depth):
        far = far0.at[k] if k < half else far1.at[k - half]
        for by, ref in ((0, own.at[k]), (3, right.at[k]), (1, left.at[k]), (2, far)):
            spot = 4 * k + jnp.bitwise_and(x + by, 3)
            yield ref, spot, pl.ds(pl.multiple_of(spot * lanes, lanes), lanes)


def unpacked(ref, start, step):
    rows, lanes = ref.shape
    half = lanes // 2
    first = ref[pl.ds(start, step), :].astype(f32)
    second = ref[pl.ds(rows // 2 + start, step), :].astype(f32)
    low = lax.broadcasted_iota(jnp.int32, (step, lanes), 1) < half
    return (
        jnp.where(low, first, pltpu.roll(second, half, 1)),
        jnp.where(low, pltpu.roll(first, half, 1), second),
    )


STEP = 48


def merge_kernel(info_ref, *refs):
    *blocks, out_ref = refs
    live, first = info_ref[1], info_ref[2]
    _, rows, lanes = blocks[0].shape

    @pl.loop(0, rows // 2 // STEP)
    def _(i):
        start = pl.multiple_of(i * STEP, STEP)
        slot = lax.broadcasted_iota(jnp.int32, (STEP, lanes), 0) + first + start
        for ref, _, here in laid_out(info_ref, blocks):
            for side, v in enumerate(unpacked(ref, start, STEP)):
                base = side * (rows // 2)
                v = jnp.where(slot + base < live, v, 0.0)
                out_ref[pl.ds(pl.multiple_of(base + start, STEP), STEP), here] = v.astype(bf16)


def norm_kernel(info_ref, *refs):
    *blocks, gain_ref, bias_ref, out_ref = refs
    _, rows, lanes = blocks[0].shape
    full = out_ref.shape[1]

    @pl.loop(0, rows // 2 // STEP)
    def _(i):
        start = pl.multiple_of(i * STEP, STEP)
        here = [pl.ds(pl.multiple_of(start + s * (rows // 2), STEP), STEP) for s in range(2)]
        zeros = jnp.zeros((STEP, lanes), f32)
        total, square = [zeros, zeros], [zeros, zeros]
        for ref, _, columns in laid_out(info_ref, blocks):
            for side, v in enumerate(unpacked(ref, start, STEP)):
                total[side] += v
                square[side] += v * v
                out_ref[here[side], columns] = v.astype(bf16)
        for side in range(2):
            mean = jnp.sum(total[side], axis=1, keepdims=True) / full
            power = jnp.sum(square[side], axis=1, keepdims=True) / full
            scale = lax.rsqrt(power - mean * mean + epsilon)
            for k in range(full // lanes):
                columns = slice(k * lanes, (k + 1) * lanes)
                v = (out_ref[here[side], columns].astype(f32) - mean) * scale
                v = v * gain_ref[k:k + 1, :] + bias_ref[k:k + 1, :]
                out_ref[here[side], columns] = v.astype(bf16)


def assemble(kernel, name, info, blocks, extra=()):
    depth, rows, lanes = blocks[0].shape
    return pl.pallas_call(
        kernel,
        in_specs=[pl.BlockSpec(memory_space=pltpu.SMEM)]
        + [pl.BlockSpec(memory_space=pltpu.VMEM)] * (len(blocks) + len(extra)),
        out_specs=pl.BlockSpec(memory_space=pltpu.VMEM),
        out_shape=jax.ShapeDtypeStruct((rows, 4 * depth * lanes), bf16),
        compiler_params=pltpu.CompilerParams(vmem_limit_bytes=32 * MIB),
        name=name,
    )(info, *blocks, *extra)


def stage_kernel(table_ref, position_ref, first, second, out, come, leave, come_sem, leave_sem):
    units, width = first.shape
    half, step = units // 2, width // 4
    replicas = table_ref.shape[1]
    chosen = jnp.int32(replicas)
    for p in reversed(range(replicas)):
        chosen = jnp.where(table_ref[1, p] == 1, p, chosen)
    copies = []
    for k in range(4):
        columns = pl.ds(k * step, step)
        for j, source in enumerate((first, second)):
            copies.append(
                pltpu.make_async_copy(source.at[:, columns], come.at[k, j], come_sem.at[k, j])
            )
            copies[-1].start()
    leaving = []
    for k in range(4):
        for j in range(2):
            copies[2 * k + j].wait()
            for c in range(2):
                kept = come[k, j, c * half:(c + 1) * half, :].astype(f32)
                kept = jnp.where(chosen == position_ref[0], kept, 0.0)
                leave[2 * k + c, j * half:(j + 1) * half, :] = kept.astype(bf16)
        block = pl.ds(2 * k, 2)
        leaving.append(pltpu.make_async_copy(leave.at[block], out.at[block], leave_sem.at[k]))
        leaving[k].start()
    for copy in leaving:
        copy.wait()


def stage(table, position, first, second):
    units, width = first.shape
    return pl.pallas_call(
        stage_kernel,
        in_specs=[pl.BlockSpec(memory_space=pltpu.SMEM)] * 2
        + [pl.BlockSpec(memory_space=pl.ANY)] * 2,
        out_specs=pl.BlockSpec(memory_space=pl.ANY),
        out_shape=jax.ShapeDtypeStruct((8, units, width // 4), bf16),
        scratch_shapes=[
            pltpu.VMEM((4, 2, units, width // 4), bf16),
            pltpu.VMEM((8, units, width // 4), bf16),
            pltpu.SemaphoreType.DMA((4, 2)),
            pltpu.SemaphoreType.DMA((4,)),
        ],
        compiler_params=pltpu.CompilerParams(vmem_limit_bytes=60 * MIB),
        name="stage",
    )(table, position, first, second)


def gradient_kernel(
    normed0, normed1, up0, up1, weights, out, rows0, rows1, rows2, rows3, held, done, acc, factors,
    come, go,
):
    units, step = weights.shape[1:]
    rows = normed0.shape[0]
    tokens = ((rows0, rows2), (rows1, rows3))
    half = units // 2
    main = 256

    copies = []
    for k in range(4):
        columns = pl.ds(k * step, step)
        pairs = [(weights.at[pl.ds(2 * k, 2)], held.at[pl.ds(2 * k, 2)])]
        for source, target in ((normed0, rows0), (normed1, rows1), (up0, rows2), (up1, rows3)):
            pairs.append((source.at[:, columns], target.at[:, columns]))
        copies.append(
            [pltpu.make_async_copy(a, b, come.at[k, n]) for n, (a, b) in enumerate(pairs)]
        )
        for copy in copies[k]:
            copy.start()

    for k in range(4):
        for copy in copies[k]:
            copy.wait()
        for j in range(2):
            both = jnp.concatenate(
                [held[2 * k + y, j * half:(j + 1) * half, :] for y in range(2)]
            )
            for t, refs in enumerate(tokens):
                here = (j, slice(t * rows, (t + 1) * rows))
                term = lax.dot_general(
                    refs[j][:, k * step:(k + 1) * step], both, (((1,), (1,)), ((), ())),
                    preferred_element_type=f32,
                )
                acc[here] = term if k == 0 else acc[here] + term

    value = acc[0]
    bent = jnp.tanh(SLOPE * (value + CUBE * value * value * value))
    slope = 0.5 * (1.0 + bent) + 0.5 * value * (1.0 - bent * bent) * (
        SLOPE * (1.0 + 3.0 * CUBE * value * value)
    )
    factors[0] = jnp.transpose(acc[1] * slope).astype(bf16)
    factors[1] = jnp.transpose(0.5 * value * (1.0 + bent)).astype(bf16)

    leaving = []
    for q in range(4):
        columns = slice(q * step, (q + 1) * step)
        for j in range(2):
            ends = [factors[j, :, main:rows], factors[j, :, rows + main:]]
            total = jnp.dot(
                jnp.concatenate(ends, axis=1),
                jnp.concatenate([refs[j][main:, columns] for refs in tokens]),
                preferred_element_type=f32,
            )
            for t, refs in enumerate(tokens):
                total += jnp.dot(
                    factors[j, :, t * rows:t * rows + main], refs[j][:main, columns],
                    preferred_element_type=f32,
                )
            total = total.astype(bf16)
            for y in range(2):
                done[2 * q + y, j] = total[y * half:(y + 1) * half]
        block = pl.ds(2 * q, 2)
        leaving.append(pltpu.make_async_copy(done.at[block], out.at[block], go.at[q]))
        leaving[q].start()
    for copy in leaving:
        copy.wait()


def gradients(normed, normed_other, upstream, upstream_other, weights):
    units, step = weights.shape[1:]
    rows, width = normed.shape
    shape = (8, 2, units // 2, step)
    return pl.pallas_call(
        gradient_kernel,
        in_specs=[pl.BlockSpec(memory_space=pl.ANY)] * 5,
        out_specs=pl.BlockSpec(memory_space=pl.ANY),
        out_shape=jax.ShapeDtypeStruct(shape, bf16),
        scratch_shapes=[pltpu.VMEM((rows, width), bf16)] * 4
        + [
            pltpu.VMEM(weights.shape, bf16),
            pltpu.VMEM(shape, bf16),
            pltpu.VMEM((2, 2 * rows, units), f32),
            pltpu.VMEM((2, units, 2 * rows), bf16),
            pltpu.SemaphoreType.DMA((4, 5)),
            pltpu.SemaphoreType.DMA((4,)),
        ],
        compiler_params=pltpu.CompilerParams(vmem_limit_bytes=56 * MIB),
        name="gradients",
    )(normed, normed_other, upstream, upstream_other, weights)


def gather_z(block):
    depth = lax.axis_size("z")
    return lax.all_to_all(jnp.broadcast_to(block, (depth,) + block.shape), "z", 0, 0)


def gather_x(own):
    return shift(own, "x", 4, 1), shift(own, "x", 4, -1)


def gather_far(right, left):
    half = right.shape[0] // 2
    return shift(right[:half], "x", 4, 1), shift(left[half:], "x", 4, -1)


def on_device(
    token_ids, replica_table, embedding, ln_gain, ln_bias, weight_in, weight_out, cotangent
):
    replicas = replica_table.shape[0]
    tok = cotangent.shape[1]
    cols = cotangent.shape[2]
    half = tok // 2
    vocab_block = embedding.shape[0]
    units, width = weight_in.shape[1:]
    part = units // 2

    yh, core, x, yl = (lax.axis_index(a) for a in ("yh", "core", "x", "yl"))
    position = 2 * yh + core
    replica_index = jnp.arange(replicas, dtype=jnp.int32)
    source = jnp.min(jnp.where(replica_table[:, 1] == 1, replica_index, replicas))
    live_counts = tok * (4 + replica_table[:, 0]) // 6
    live = lax.dynamic_index_in_dim(live_counts, position, 0, keepdims=False)

    staged = stage(replica_table.T, position.reshape(1), weight_in[0], weight_out[0])
    share_w = lax.psum_scatter(
        staged.reshape(8 * units, width // 4), ("yh", "core"), scatter_dimension=0, tiled=True
    )

    cot = cotangent[0].reshape(2, 2, half // 2, cols)
    cot = jnp.concatenate([cot[:, 0], cot[:, 1]], axis=2)
    cot = jnp.broadcast_to(cot, (8,) + cot.shape).reshape((16,) + cot.shape[1:])

    vectors = jnp.concatenate([ln_gain.reshape(-1, 2 * cols), ln_bias.reshape(-1, 2 * cols)])
    share = vectors.shape[0] // 2
    held = jnp.concatenate([embedding.T, vectors], axis=1)
    ids = token_ids.reshape(4, 2, 2, 2, half // 2)
    ids = jnp.where(core == 0, ids[:, 0], ids[:, 1])
    local = jnp.bitwise_xor(ids - yh * 2 * vocab_block, core * vocab_block)
    low = local[:, :, 0].reshape(-1, 1)
    high = local[:, :, 1].reshape(-1, 1)

    info = jnp.stack([x, live, yl * half]).astype(jnp.int32)

    def slots(low, high, held, cot):
        cot = lax.all_to_all(cot, ("z", "yl"), 0, 0).reshape(8, half, 2 * cols)
        swapped = shift(held, "core", 2, 1)
        rows = lookup(low, high, held, swapped, vocab_block // 8).reshape(8, half // 2, 2 * cols)
        vectors = jnp.where(core == source % 2, held[:, vocab_block:], swapped[:, vocab_block:])
        vectors = lax.dynamic_slice_in_dim(vectors, yl * share, share, 0)
        sent = jnp.concatenate([rows, jnp.broadcast_to(vectors, (8,) + vectors.shape)], axis=1)
        sent, cot = lax.optimization_barrier((sent, cot))
        got = lax.all_to_all(sent, ("yh", "yl"), 0, 0)
        got, sides = lax.optimization_barrier((got, gather_x(cot)))
        far = gather_far(*sides)
        got = got.reshape((4, 2) + got.shape[1:])
        emb = jnp.sum(got[:, :, : half // 2].astype(f32), axis=0).astype(bf16)
        emb = emb.reshape(half, 2 * cols)
        root = lax.dynamic_index_in_dim(got[:, :, half // 2 :], source // 2, 0, keepdims=False)
        root = root.reshape(2, -1, 2 * cols).astype(f32)
        return (root[0], root[1], gather_z(emb), cot, *sides, *far)

    def no_slots(low, high, held, cot):
        lanes = 2 * cols
        vector, blocks = jnp.zeros((width // lanes, lanes), f32), jnp.zeros((8, half, lanes), bf16)
        return (vector, vector) + (blocks,) * 4 + (blocks[:4],) * 2

    def features(gain, bias, emb, *cot):
        upstream = assemble(merge_kernel, "merge", info, cot)
        sides, upstream = lax.optimization_barrier((gather_x(emb), upstream))
        blocks = (emb, *sides, *gather_far(*sides))
        normed = assemble(norm_kernel, "norm", info, blocks, (gain, bias))
        return normed, shift(normed, "core", 2, 1), upstream, shift(upstream, "core", 2, 1)

    def no_features(*blocks):
        return (jnp.zeros((half, width), bf16),) * 4

    some = source < replicas
    blocks = lax.cond(some, slots, no_slots, low, high, held, cot)
    *blocks, share_w = lax.optimization_barrier((*blocks, share_w))
    weights = lax.all_gather(share_w, ("yh", "yl"), tiled=True).reshape(8, units, width // 4)
    normed, normed_other, upstream, upstream_other = lax.cond(some, features, no_features, *blocks)
    terms = gradients(normed, normed_other, upstream, upstream_other, weights)
    terms = terms.reshape(16, part, width // 4)
    sums = lax.psum_scatter(terms, ("yh", "yl"), scatter_dimension=0, tiled=True)
    left, right = sums[:, :, : width // 8], sums[:, :, width // 8 :]
    theirs = shift(jnp.where(core == 0, right, left), "core", 2, 1)
    mine = jnp.where(core == 0, left, right)
    top = jnp.where(core == 0, mine, theirs)
    bottom = jnp.where(core == 0, theirs, mine)
    done = jnp.concatenate([top, bottom], axis=1)
    return done[0], done[1]


def solution(mesh):
    fine = Mesh(mesh.devices.reshape(4, 2, 8, 4, 2), ("yh", "core", "z", "x", "yl"))
    pipe, mp = ("yh", "core"), ("z", "x", "yl")
    placed = (
        P(),
        P(),
        P(pipe, mp),
        P(pipe, None),
        P(pipe, None),
        P(pipe, mp, None),
        P(pipe, mp, None),
        P(pipe, None, mp),
    )
    return jax.shard_map(
        on_device,
        mesh=fine,
        in_specs=placed,
        out_specs=(P(mp, pipe), P(mp, pipe)),
        check_vma=False,
    )
```
